32 devices in a mesh: node: 8 (over z, core), local: 4 (over y, x).
Axes of the slice: x: 2, y: 2, z: 4, core: 2. Of those that a mesh axis runs over, the one named last changes fastest.
Arguments:
- tokens: bfloat16 [512, 4096], P('local', 'node'), may hold values from -6 to 6
- gate_up_codes: bfloat16 [2, 4096, 14336], P(None, 'local', 'node'), may hold values from -127 to 127
- gate_up_scales: bfloat16 [2, 32, 14336], P(None, 'local', 'node'), may hold values from 2.9921532e-05 to 0.00029945374
- d_hidden: bfloat16 [512, 14336], P('local', 'node'), may hold values from -6 to 6
Outputs:
- hidden: bfloat16 [512, 14336], P('local', 'node')
- d_tokens: bfloat16 [512, 4096], P('local', 'node')
- grad_gate_up: float32 [2, 4096, 14336], P(None, 'local', 'node')
The draws below stay inside these ranges and needn't reach their ends.
All inputs are finite; a program needn't handle non-finite values.
Results may differ from the reference program's by a relative error of at most 0.023.
Values may be sent and summed in bfloat16 or wider, within the bound.
No kernel may reach another device: no remote copies, remote signals or barrier semaphores. Data moves between devices by JAX's collectives and lax.ppermute only.
A program may use at most 128 MiB of HBM per device.

```python
import math
import jax
import jax.numpy as jnp
from jax import lax

D = 4096
FF = 14336
BLOCK = 128
TOK_DEV = 128
TOKENS = 512
N_NODE = 8
N_LOCAL = 4


def level_of(rng, shape, shards, low, largest):
    gain = 1.0
    for position, blocks in shards:
        heights = jax.random.uniform(jax.random.fold_in(jax.random.fold_in(rng, 6), position), (blocks,), jnp.float32, low / len(shards), largest / len(shards))
        gain = gain * jnp.repeat(jnp.exp(heights), shape[position] // blocks).reshape((-1,) + (1,) * (len(shape) - 1 - position))
    return gain


def gaussian(rng, extent, deviation, most, cuts=(), kind=jnp.bfloat16):
    entries = deviation * jax.random.normal(rng, extent, jnp.float32)
    if cuts:
        entries = entries * level_of(rng, extent, cuts, -0.22, 0.18)
    return jnp.clip(entries, -most, most).astype(kind)


def setup_inputs(seed: int = 0) -> dict:
    key_of = jax.random.split(jax.random.key(seed), 5)
    return {
        "tokens": gaussian(key_of[0], (TOKENS, D), 1.0, 6.0, ((0, 4), (1, 8))),
        "gate_up_codes": jnp.clip(jax.random.uniform(key_of[1], (2, D, FF), jnp.float32, -127.0, 127.0) * level_of(key_of[1], (2, D, FF), ((1, 4), (2, 8)), -0.4, 0.0), -127.0, 127.0).astype(jnp.bfloat16),
        "gate_up_scales": jnp.clip(jnp.exp(math.log(0.00029945374) - 2.3033816 * jax.random.uniform(key_of[2], (2, D // BLOCK, FF), jnp.float32) ** level_of(key_of[2], (2, D // BLOCK, FF), ((1, 4), (2, 8)), -0.2, 0.2)), 2.9921531677246094e-05, 0.00029945374).astype(jnp.bfloat16),
        "d_hidden": gaussian(key_of[3], (TOKENS, FF), 1.0, 6.0, ((0, 4), (1, 8))),
    }


def dequant(codes, scales):
    shape = codes.shape
    blocked = codes.astype(jnp.float32).reshape(shape[:-2] + (shape[-2] // BLOCK, BLOCK, shape[-1]))
    weight = blocked * scales.astype(jnp.float32)[..., :, None, :]
    return weight.reshape(shape).astype(jnp.bfloat16)

def reference(tokens, gate_up_codes, gate_up_scales, d_hidden):
    w_gu = dequant(gate_up_codes, gate_up_scales)
    gate = jnp.dot(tokens, w_gu[0], preferred_element_type=jnp.float32)
    up = jnp.dot(tokens, w_gu[1], preferred_element_type=jnp.float32)
    sigmoid_gate = jax.nn.sigmoid(gate)
    active = gate * sigmoid_gate
    hidden = (active * up).astype(jnp.bfloat16)
    grad_in = d_hidden.astype(jnp.float32)
    d_gate = (grad_in * up * sigmoid_gate * (1.0 + gate * (1.0 - sigmoid_gate))).astype(jnp.bfloat16)
    d_up = (grad_in * active).astype(jnp.bfloat16)
    group = FF // N_NODE
    gate_groups = d_gate.reshape(TOKENS, N_NODE, group).transpose(1, 0, 2)
    up_groups = d_up.reshape(TOKENS, N_NODE, group).transpose(1, 0, 2)
    wg_groups = w_gu[0].reshape(D, N_NODE, group).transpose(1, 0, 2)
    wu_groups = w_gu[1].reshape(D, N_NODE, group).transpose(1, 0, 2)

    def node_step(carry, pieces):
        dg, du, wg, wu = pieces
        term = lax.dot_general(dg, wg, (((1,), (1,)), ((), ())), preferred_element_type=jnp.float32)
        term = term + lax.dot_general(du, wu, (((1,), (1,)), ((), ())), preferred_element_type=jnp.float32)
        rounded = lax.optimization_barrier(term.astype(jnp.bfloat16))
        return (carry + rounded.astype(jnp.float32), None)
    token_sum, _ = lax.scan(node_step, jnp.zeros((TOKENS, D), jnp.float32), (gate_groups, up_groups, wg_groups, wu_groups))
    d_tokens = token_sum.astype(jnp.bfloat16)
    factor = 1.0 / math.sqrt(TOKENS)
    xs = tokens.reshape(N_LOCAL, TOK_DEV, D)
    gs = d_gate.reshape(N_LOCAL, TOK_DEV, FF)
    us = d_up.reshape(N_LOCAL, TOK_DEV, FF)

    def block_step(carry, pieces):
        rows, dg, du = pieces
        first = lax.dot_general(rows, dg, (((0,), (0,)), ((), ())), preferred_element_type=jnp.float32)
        second = lax.dot_general(rows, du, (((0,), (0,)), ((), ())), preferred_element_type=jnp.float32)
        partial_value = lax.optimization_barrier(jnp.stack([first, second]).astype(jnp.bfloat16))
        return (carry + partial_value.astype(jnp.float32), None)
    grads, _ = lax.scan(block_step, jnp.zeros((2, D, FF), jnp.float32), (xs, gs, us))
    return (hidden, d_tokens, grads * factor)
```

```python
import math

import jax
import jax.numpy as jnp
from jax import lax
from jax.sharding import PartitionSpec as P

BLOCK = 128


def dequant(codes, scales):
    shape = codes.shape
    blocked = codes.astype(jnp.float32).reshape(shape[:-2] + (shape[-2] // BLOCK, BLOCK, shape[-1]))
    weight = blocked * scales.astype(jnp.float32)[..., :, None, :]
    return weight.reshape(shape).astype(jnp.bfloat16)


def swap(nodes, locals_):
    ratio = nodes // locals_
    pairs = []
    for a in range(locals_):
        for h in range(ratio):
            for b in range(locals_):
                pairs.append(((ratio * a + h) * locals_ + b, (ratio * b + h) * locals_ + a))
    return pairs


def body(tokens, gate_up_codes, gate_up_scales, d_hidden):
    rows, feats = tokens.shape
    nodes, locals_ = lax.axis_size("node"), lax.axis_size("local")
    ratio = nodes // locals_
    _, owned, group = gate_up_codes.shape
    pairs = swap(nodes, locals_)
    total = rows * locals_

    mine = lax.ppermute(tokens, ("node", "local"), pairs)
    pieces = lax.all_gather(mine, "node", axis=0)
    features = pieces.reshape(locals_, ratio, rows, feats).transpose(0, 2, 1, 3).reshape(total, owned)

    w_gu = dequant(gate_up_codes, gate_up_scales)
    partial = lax.dot_general(
        features, w_gu, (((1,), (1,)), ((), ())), preferred_element_type=jnp.float32
    ).astype(jnp.bfloat16)
    both = lax.psum_scatter(partial, "local", scatter_dimension=0, tiled=True).astype(jnp.float32)
    gate, up = both[:, 0], both[:, 1]
    sigmoid_gate = jax.nn.sigmoid(gate)
    active = gate * sigmoid_gate
    hidden = (active * up).astype(jnp.bfloat16)
    grad_in = d_hidden.astype(jnp.float32)
    d_gate = (grad_in * up * sigmoid_gate * (1.0 + gate * (1.0 - sigmoid_gate))).astype(jnp.bfloat16)
    d_up = (grad_in * active).astype(jnp.bfloat16)
    d_both = lax.all_gather(jnp.stack([d_gate, d_up], axis=1), "local", axis=0, tiled=True)

    term = lax.dot_general(
        d_both, w_gu, (((1, 2), (0, 2)), ((), ())), preferred_element_type=jnp.float32
    ).astype(jnp.bfloat16)
    term = term.reshape(locals_, rows, ratio, feats).transpose(0, 2, 1, 3).reshape(nodes * rows, feats)
    summed = lax.psum_scatter(term, "node", scatter_dimension=0, tiled=True)
    d_tokens = lax.ppermute(summed, ("node", "local"), pairs)

    grads = lax.dot_general(
        features, d_both, (((0,), (0,)), ((), ())), preferred_element_type=jnp.float32
    ) * (1.0 / math.sqrt(total))
    return (hidden, d_tokens, grads.transpose(1, 0, 2))


def solution(mesh):
    placed = (
        P("local", "node"),
        P(None, "local", "node"),
        P(None, "local", "node"),
        P("local", "node"),
    )
    return jax.shard_map(
        body,
        mesh=mesh,
        in_specs=placed,
        out_specs=(P("local", "node"), P("local", "node"), P(None, "local", "node")),
        check_vma=False,
    )
```

```python
import functools
import math

import jax
import jax.numpy as jnp
from jax import lax
from jax.experimental import pallas as pl
from jax.experimental.pallas import tpu as pltpu
from jax.sharding import PartitionSpec as P

BLOCK = 128
CHUNKS = 2
AXES = ("node", "local")


def dequant(codes, scales):
    shape = codes.shape
    blocked = codes.astype(jnp.float32).reshape(shape[:-2] + (shape[-2] // BLOCK, BLOCK, shape[-1]))
    weight = blocked * scales.astype(jnp.float32)[..., :, None, :]
    return weight.reshape(shape).astype(jnp.bfloat16)


def pairs(move, places, ratio):
    out = []
    for plane in range(places):
        for half in range(ratio):
            for place in range(places):
                p, h, q = move(plane, half, place)
                out.append(
                    ((plane * ratio + half) * places + place, (p * ratio + h) * places + q)
                )
    return out


def reorder(x, mask, axis=0):
    size = x.shape[axis]
    return jnp.concatenate(
        [lax.dynamic_slice_in_dim(x, i ^ mask, 1, axis) for i in range(size)], axis=axis
    )


def weight_grad_kernel(scale, features_ref, d_ref, out_ref):
    out_ref[0] = scale * lax.dot_general(
        features_ref[...], d_ref[0], (((0,), (0,)), ((), ())), preferred_element_type=jnp.float32
    )


def weight_grad(features, d_both, scale):
    total, owned = features.shape
    group = d_both.shape[2]
    step = min(owned, 256)
    return pl.pallas_call(
        functools.partial(weight_grad_kernel, scale),
        grid=(2, owned // step),
        in_specs=[
            pl.BlockSpec((total, step), lambda g, i: (0, i)),
            pl.BlockSpec((1, total, group), lambda g, i: (g, 0, 0)),
        ],
        out_specs=pl.BlockSpec((1, step, group), lambda g, i: (g, i, 0)),
        out_shape=jax.ShapeDtypeStruct((2, owned, group), jnp.float32),
        compiler_params=pltpu.CompilerParams(vmem_limit_bytes=40 * 1024 * 1024),
    )(features, d_both)


def body(tokens, gate_up_codes, gate_up_scales, d_hidden):
    rows, feats = tokens.shape
    nodes, places = lax.axis_size("node"), lax.axis_size("local")
    ratio = nodes // places
    _, owned, group = gate_up_codes.shape
    bits = [1 << b for b in range(places.bit_length() - 1)]
    node, place = lax.axis_index("node"), lax.axis_index("local")
    plane, half = node // ratio, node % ratio
    mask = plane ^ place
    chunk = rows // CHUNKS
    part = chunk // 2

    def permute(x, move):
        return lax.ppermute(x, AXES, pairs(move, places, ratio))

    def features_of(x):
        got = jnp.stack(
            [permute(x, lambda p, h, q, j=j: (q ^ j, h, p)) for j in range(places)]
        )
        halves = jnp.stack(
            [got] + [permute(got, lambda p, h, q, e=e: (p, h ^ e, q)) for e in range(1, ratio)]
        )
        halves = reorder(reorder(halves, half, 0), mask, 1)
        return halves.transpose(1, 2, 0, 3).reshape(places, x.shape[0], owned)

    def reduce_local(x, order):
        ks = list(range(places))
        x = x.astype(jnp.float32)
        for bit in order:
            away = [i for i, k in enumerate(ks) if k & bit]
            stay = [i for i, k in enumerate(ks) if not k & bit]
            sent = jnp.stack([x[:, i] for i in away], axis=1).astype(jnp.bfloat16)
            got = permute(sent, lambda p, h, q: (p, h, q ^ bit))
            x = jnp.stack([x[:, i] for i in stay], axis=1) + got.astype(jnp.float32)
            ks = [ks[i] for i in stay]
        return x[:, 0]

    def gather_local(x, order):
        x, ks = x[:, None], [0]
        for bit in order:
            got = permute(x, lambda p, h, q: (p, h, q ^ bit))
            x = jnp.concatenate([x, got], axis=1)
            ks = ks + [k ^ bit for k in ks]
        return x, ks

    w_gu = dequant(gate_up_codes, gate_up_scales)
    hidden, all_features, all_d, d_tokens = [], [], [], []
    for c in range(CHUNKS):
        features = features_of(tokens[c * chunk : (c + 1) * chunk])
        flat = features.reshape(places * chunk, owned)
        partial = [
            jnp.dot(flat, w_gu[g], preferred_element_type=jnp.float32)
            .astype(jnp.bfloat16)
            .reshape(places, chunk, group)
            for g in range(2)
        ]
        gathered = []
        for s in range(2):
            order = bits if s == 0 else bits[::-1]
            at = slice(s * part, (s + 1) * part)
            both = reduce_local(jnp.stack([p[:, at] for p in partial]), order)
            gate, up = both[0], both[1]
            sigmoid_gate = jax.nn.sigmoid(gate)
            active = gate * sigmoid_gate
            hidden.append((active * up).astype(jnp.bfloat16))
            first = c * chunk + s * part
            grad_in = d_hidden[first : first + part].astype(jnp.float32)
            d_gate = grad_in * up * sigmoid_gate * (1.0 + gate * (1.0 - sigmoid_gate))
            d_up = grad_in * active
            d_both, ks = gather_local(jnp.stack([d_gate, d_up]).astype(jnp.bfloat16), order)
            gathered.append((d_both, ks))
            all_d.append(d_both.reshape(2, places * part, group))
            all_features += [features[k, at] for k in ks]
        d_chunk = jnp.concatenate([d.reshape(2, places * part, group) for d, _ in gathered], axis=1)
        term = lax.dot_general(
            d_chunk[0], w_gu[0], (((1,), (1,)), ((), ())), preferred_element_type=jnp.float32
        ) + lax.dot_general(
            d_chunk[1], w_gu[1], (((1,), (1,)), ((), ())), preferred_element_type=jnp.float32
        )
        streams = []
        for s, (_, ks) in enumerate(gathered):
            piece = term[s * places * part : (s + 1) * places * part].reshape(places, part, ratio, feats)
            back = [ks.index(k) for k in range(places)]
            streams.append(jnp.stack([piece[i] for i in back]))
        term = jnp.concatenate(streams, axis=1)
        term = reorder(term, half, 2)
        summed = term[:, :, 0]
        for e in range(1, ratio):
            got = permute(term[:, :, e].astype(jnp.bfloat16), lambda p, h, q: (p, h ^ e, q))
            summed = summed + got.astype(jnp.float32)
        summed = summed.astype(jnp.bfloat16)
        arrived = jnp.stack(
            [summed[0]]
            + [permute(summed[k], lambda p, h, q: (p, h, q ^ k)) for k in range(1, places)]
        )
        arrived = reorder(arrived, mask, 0)
        result = arrived[0].astype(jnp.float32)
        for j in range(1, places):
            got = permute(arrived[j], lambda p, h, q: (p ^ j, h, q))
            result = result + got.astype(jnp.float32)
        d_tokens.append(result.astype(jnp.bfloat16))

    grads = weight_grad(
        jnp.concatenate(all_features), jnp.concatenate(all_d, axis=1), 1.0 / math.sqrt(rows * places)
    )
    return jnp.concatenate(hidden), jnp.concatenate(d_tokens), grads


def solution(mesh):
    placed = (
        P("local", "node"),
        P(None, "local", "node"),
        P(None, "local", "node"),
        P("local", "node"),
    )
    return jax.shard_map(
        body,
        mesh=mesh,
        in_specs=placed,
        out_specs=(P("local", "node"), P("local", "node"), P(None, "local", "node")),
        check_vma=False,
    )
```

```python
import functools
import math

import jax
import jax.numpy as jnp
from jax import lax
from jax.experimental import pallas as pl
from jax.experimental.pallas import tpu as pltpu
from jax.sharding import PartitionSpec as P

BLOCK = 128
CHUNKS = 2
AXES = ("node", "local")


def dequant(codes, scales):
    shape = codes.shape
    blocked = codes.astype(jnp.float32).reshape(shape[:-2] + (shape[-2] // BLOCK, BLOCK, shape[-1]))
    weight = blocked * scales.astype(jnp.float32)[..., :, None, :]
    return weight.reshape(shape).astype(jnp.bfloat16)


def pairs(move, places, ratio):
    out = []
    for plane in range(places):
        for half in range(ratio):
            for place in range(places):
                p, h, q = move(plane, half, place)
                out.append(
                    ((plane * ratio + half) * places + place, (p * ratio + h) * places + q)
                )
    return out


def pick(choices, index):
    out = choices[0]
    for i in range(1, len(choices)):
        out = jnp.where(index == i, choices[i], out)
    return out


def after(x, earlier):
    return lax.optimization_barrier((x, earlier))[0]


def input_grad_kernel(spots, place_ref, *refs):
    pieces, (w_ref, d_ref, term_ref) = refs[: len(spots)], refs[len(spots) :]

    @pl.when((pl.program_id(0) == 0) & (pl.program_id(1) == 0))
    def _():
        for piece, first in zip(pieces, spots):
            streams, _, part, _ = piece.shape
            for s in range(streams):
                d_ref[:, pl.ds(first + s * part, part), :] = piece[s]

    numbers = (((1,), (1,)), ((), ()))
    term = lax.dot_general(d_ref[0], w_ref[0], numbers, preferred_element_type=jnp.float32)
    term += lax.dot_general(d_ref[1], w_ref[1], numbers, preferred_element_type=jnp.float32)
    term_ref[0] = term.astype(jnp.bfloat16)


def input_grad(pieces, spots, w_gu, half, ratio, total):
    _, owned, group = w_gu.shape
    feats = owned // ratio
    step = min(feats, 256)
    blocks = feats // step
    whole = lambda x: pl.BlockSpec(x.shape, lambda e, i, place: (0,) * x.ndim)
    return pl.pallas_call(
        functools.partial(input_grad_kernel, spots),
        grid_spec=pltpu.PrefetchScalarGridSpec(
            num_scalar_prefetch=1,
            grid=(ratio, blocks),
            in_specs=[whole(x) for x in pieces]
            + [pl.BlockSpec((2, step, group), lambda e, i, place: (0, (place[0] ^ e) * blocks + i, 0))],
            out_specs=[
                pl.BlockSpec((2, total, group), lambda e, i, place: (0, 0, 0)),
                pl.BlockSpec((1, total, step), lambda e, i, place: (e, 0, i)),
            ],
        ),
        out_shape=[
            jax.ShapeDtypeStruct((2, total, group), jnp.bfloat16),
            jax.ShapeDtypeStruct((ratio, total, feats), jnp.bfloat16),
        ],
        compiler_params=pltpu.CompilerParams(vmem_limit_bytes=40 * 1024 * 1024),
    )(half[None], *pieces, w_gu)


def weight_grad_kernel(scale, *refs):
    count = (len(refs) - 1) // 2
    total = 0.0
    for features_ref, d_ref in zip(refs[:count], refs[count:-1]):
        total += lax.dot_general(
            features_ref[...], d_ref[0], (((0,), (0,)), ((), ())), preferred_element_type=jnp.float32
        )
    refs[-1][0] = scale * total


def weight_grad(features, d_both, scale):
    owned, group = features[0].shape[1], d_both[0].shape[2]
    step = min(owned, 256)
    return pl.pallas_call(
        functools.partial(weight_grad_kernel, scale),
        grid=(2, owned // step),
        in_specs=[pl.BlockSpec((f.shape[0], step), lambda g, i: (0, i)) for f in features]
        + [pl.BlockSpec((1, d.shape[1], group), lambda g, i: (g, 0, 0)) for d in d_both],
        out_specs=pl.BlockSpec((1, step, group), lambda g, i: (g, i, 0)),
        out_shape=jax.ShapeDtypeStruct((2, owned, group), jnp.float32),
        compiler_params=pltpu.CompilerParams(vmem_limit_bytes=40 * 1024 * 1024),
    )(*features, *d_both)


def body(tokens, gate_up_codes, gate_up_scales, d_hidden):
    rows, feats = tokens.shape
    nodes, places = lax.axis_size("node"), lax.axis_size("local")
    ratio = nodes // places
    _, owned, group = gate_up_codes.shape
    bits = [1 << b for b in range(places.bit_length() - 1)]
    node, place = lax.axis_index("node"), lax.axis_index("local")
    plane, half = node // ratio, node % ratio
    mask = plane ^ place
    chunk = rows // CHUNKS
    part = chunk // 2
    orders = (bits, bits[::-1])

    def permute(x, move):
        return lax.ppermute(x, AXES, pairs(move, places, ratio))

    def features_of(x):
        got = [permute(x, lambda p, h, q, j=j: (q ^ j, h, p)) for j in range(places)]
        got = jnp.stack([pick(got, k ^ mask) for k in range(places)])
        halves = [got] + [permute(got, lambda p, h, q, e=e: (p, h ^ e, q)) for e in range(1, ratio)]
        return jnp.concatenate([pick(halves, half ^ e) for e in range(ratio)], axis=2)

    def reduce_local(x, order):
        ks = list(range(places))
        x = x.astype(jnp.float32)
        for bit in order:
            away = [i for i, k in enumerate(ks) if k & bit]
            stay = [i for i, k in enumerate(ks) if not k & bit]
            sent = jnp.stack([x[:, i] for i in away], axis=1).astype(jnp.bfloat16)
            got = permute(sent, lambda p, h, q: (p, h, q ^ bit))
            x = jnp.stack([x[:, i] for i in stay], axis=1) + got.astype(jnp.float32)
            ks = [ks[i] for i in stay]
        return x[:, 0]

    def gather_local(x):
        direct = {bit: permute(x, lambda p, h, q: (p, h, q ^ bit)) for bit in bits}
        pieces, spots = [x] + [direct[bit] for bit in bits], [0] + [bit * chunk for bit in bits]
        for s, order in enumerate(orders):
            held = {0: None}
            for bit in order:
                for k in list(held):
                    if k == 0:
                        held[bit] = direct[bit][s : s + 1]
                    else:
                        held[k ^ bit] = permute(held[k], lambda p, h, q: (p, h, q ^ bit))
                        pieces.append(held[k ^ bit])
                        spots.append((k ^ bit) * chunk + s * part)
        return pieces, spots

    w_gu = dequant(gate_up_codes, gate_up_scales)
    hidden, all_features, all_d, d_tokens = [], [], [], []
    for c in range(CHUNKS):
        features = features_of(tokens[c * chunk : (c + 1) * chunk])
        flat = features.reshape(places * chunk, owned)
        all_features.append(flat)
        partial = [
            jnp.dot(flat, w_gu[g], preferred_element_type=jnp.float32)
            .astype(jnp.bfloat16)
            .reshape(places, chunk, group)
            for g in range(2)
        ]
        streams = []
        for s in range(2):
            at = slice(s * part, (s + 1) * part)
            both = reduce_local(jnp.stack([p[:, at] for p in partial]), orders[s])
            gate, up = both[0], both[1]
            sigmoid_gate = jax.nn.sigmoid(gate)
            active = gate * sigmoid_gate
            hidden.append((active * up).astype(jnp.bfloat16))
            first = c * chunk + s * part
            grad_in = d_hidden[first : first + part].astype(jnp.float32)
            d_gate = grad_in * up * sigmoid_gate * (1.0 + gate * (1.0 - sigmoid_gate))
            d_up = grad_in * active
            streams.append(jnp.stack([d_gate, d_up]).astype(jnp.bfloat16))
        pieces, spots = gather_local(jnp.stack(streams))
        d_all, term = input_grad(pieces, spots, w_gu, half, ratio, places * chunk)
        all_d.append(d_all)
        summed = term[0].astype(jnp.float32)
        for e in range(1, ratio):
            got = permute(term[e], lambda p, h, q: (p, h ^ e, q))
            summed = summed + got.astype(jnp.float32)
        summed = summed.astype(jnp.bfloat16).reshape(places, chunk, feats)
        arrived = [summed[0]] + [
            permute(summed[k], lambda p, h, q: (p, h, q ^ k)) for k in range(1, places)
        ]
        arrived = [pick(arrived, j ^ mask) for j in range(places)]
        result = arrived[0].astype(jnp.float32)
        for j in range(1, places):
            got = permute(arrived[j], lambda p, h, q: (p ^ j, h, q))
            result = result + got.astype(jnp.float32)
        d_tokens.append(result.astype(jnp.bfloat16))

    grads = weight_grad(all_features, all_d, 1.0 / math.sqrt(rows * places))
    return jnp.concatenate(hidden), jnp.concatenate(d_tokens), grads


def solution(mesh):
    placed = (
        P("local", "node"),
        P(None, "local", "node"),
        P(None, "local", "node"),
        P("local", "node"),
    )
    return jax.shard_map(
        body,
        mesh=mesh,
        in_specs=placed,
        out_specs=(P("local", "node"), P("local", "node"), P(None, "local", "node")),
        check_vma=False,
    )
```

```python
import functools
import math

import jax
import jax.numpy as jnp
from jax import lax
from jax.experimental import pallas as pl
from jax.experimental.pallas import tpu as pltpu
from jax.sharding import PartitionSpec as P

BLOCK = 128
CHUNKS = 2
AXES = ("node", "local")


def in_vmem(x):
    return pltpu.with_memory_space_constraint(x, pltpu.VMEM)


def dequant_kernel(codes_ref, scales_ref, w_ref, done_ref):
    done_ref[0] = 0
    row = pl.ds(pl.program_id(0), 1)
    for g in range(2):
        w_ref[g] = (codes_ref[g].astype(jnp.float32) * scales_ref[g, row, :]).astype(jnp.bfloat16)


def dequant(codes, scales):
    _, owned, group = codes.shape
    blocks = owned // BLOCK
    return pl.pallas_call(
        dequant_kernel,
        grid=(blocks,),
        in_specs=[
            pl.BlockSpec((2, BLOCK, group), lambda i: (0, i, 0)),
            pl.BlockSpec((2, blocks, group), lambda i: (0, 0, 0)),
        ],
        out_specs=[
            pl.BlockSpec((2, BLOCK, group), lambda i: (0, i, 0)),
            pl.BlockSpec(memory_space=pltpu.SMEM),
        ],
        out_shape=[
            pltpu.VMEM(codes.shape, jnp.bfloat16),
            jax.ShapeDtypeStruct((1,), jnp.int32),
        ],
        compiler_params=pltpu.CompilerParams(vmem_limit_bytes=16 * 1024 * 1024),
    )(pltpu.with_memory_space_constraint(codes, pltpu.HBM), scales.astype(jnp.float32))


def pairs(move, places, ratio):
    out = []
    for plane in range(places):
        for half in range(ratio):
            for place in range(places):
                p, h, q = move(plane, half, place)
                out.append(
                    ((plane * ratio + half) * places + place, (p * ratio + h) * places + q)
                )
    return out


def after(x, earlier):
    return lax.optimization_barrier((x, earlier))[0]


def shuffle_kernel(count, write, index_ref, *refs):
    choices, outs = refs[:count], refs[-1:] if write else refs[-count:]
    for i in range(count):
        for j in range(count):

            @pl.when(index_ref[0] == i ^ j)
            def _():
                if write:
                    write(outs[0], i, choices[j][...])
                else:
                    outs[i][...] = choices[j][...]


def shuffle(choices, index, earlier=(), shape=None, write=None):
    one = choices[0]
    shapes = [shape] if write else [one.shape] * len(choices)
    out = pl.pallas_call(
        functools.partial(shuffle_kernel, len(choices), write),
        in_specs=[pl.BlockSpec(memory_space=pltpu.SMEM)]
        + [pl.BlockSpec(memory_space=pltpu.VMEM)] * len(choices)
        + [pl.BlockSpec(memory_space=pl.ANY)] * len(earlier),
        out_specs=[pl.BlockSpec(memory_space=pltpu.VMEM)] * len(shapes),
        out_shape=[pltpu.VMEM(s, one.dtype) for s in shapes],
        compiler_params=pltpu.CompilerParams(vmem_limit_bytes=16 * 1024 * 1024),
    )(index, *[in_vmem(x) for x in choices], *earlier)
    return out[0] if write else list(out)


def input_grad_kernel(spots, half_ref, *refs):
    pieces, w_ref, d_ref = refs[: len(spots)], refs[len(spots)], refs[len(spots) + 1]
    term_refs = refs[len(spots) + 2 :]
    for piece, first in zip(pieces, spots):
        streams, _, part, _ = piece.shape
        for s in range(streams):
            d_ref[:, pl.ds(first + s * part, part), :] = piece[s]
    numbers = (((1,), (1,)), ((), ()))
    for e, term_ref in enumerate(term_refs):
        feats = term_ref.shape[1]
        rows = pl.ds(pl.multiple_of((half_ref[0] ^ e) * feats, feats), feats)
        term = lax.dot_general(d_ref[0], w_ref[0, rows, :], numbers, preferred_element_type=jnp.float32)
        term += lax.dot_general(d_ref[1], w_ref[1, rows, :], numbers, preferred_element_type=jnp.float32)
        term_ref[...] = term.astype(jnp.bfloat16)


def input_grad(pieces, spots, w_gu, half, ratio, total):
    _, owned, group = w_gu.shape
    feats = owned // ratio
    return pl.pallas_call(
        functools.partial(input_grad_kernel, spots),
        in_specs=[pl.BlockSpec(memory_space=pltpu.SMEM)]
        + [pl.BlockSpec(memory_space=pltpu.VMEM)] * (len(pieces) + 1),
        out_specs=[pl.BlockSpec(memory_space=pltpu.VMEM)] * (ratio + 1),
        out_shape=[pltpu.VMEM((2, total, group), jnp.bfloat16)]
        + [pltpu.VMEM((total, feats), jnp.bfloat16)] * ratio,
        compiler_params=pltpu.CompilerParams(vmem_limit_bytes=24 * 1024 * 1024),
    )(half, *[in_vmem(x) for x in pieces], in_vmem(w_gu))


def weight_grad_kernel(scale, features_ref, d_ref, *refs):
    out_ref, done_ref = refs[-2:]
    done_ref[0] = 0
    out_ref[0] = scale * jnp.dot(features_ref[...], d_ref[0], preferred_element_type=jnp.float32)


def weight_grad(which, features, d_both, scale, earlier, grads=None):
    owned, total = features.shape
    group = d_both.shape[2]
    step = min(owned, 256)
    operands = [features, in_vmem(d_both), earlier] + ([] if grads is None else [grads])
    return pl.pallas_call(
        functools.partial(weight_grad_kernel, scale),
        grid=(owned // step,),
        in_specs=[
            pl.BlockSpec((step, total), lambda i: (i, 0)),
            pl.BlockSpec((1, total, group), lambda i: (which, 0, 0)),
        ]
        + [pl.BlockSpec(memory_space=pl.ANY)] * (len(operands) - 2),
        out_specs=[
            pl.BlockSpec((1, step, group), lambda i: (which, i, 0)),
            pl.BlockSpec(memory_space=pltpu.SMEM),
        ],
        out_shape=[
            jax.ShapeDtypeStruct((2, owned, group), jnp.float32),
            jax.ShapeDtypeStruct((1,), jnp.int32),
        ],
        input_output_aliases={} if grads is None else {3: 0},
        compiler_params=pltpu.CompilerParams(vmem_limit_bytes=16 * 1024 * 1024),
    )(*operands)


def body(tokens, gate_up_codes, gate_up_scales, d_hidden):
    rows, feats = tokens.shape
    nodes, places = lax.axis_size("node"), lax.axis_size("local")
    ratio = nodes // places
    _, owned, group = gate_up_codes.shape
    bits = [1 << b for b in range(places.bit_length() - 1)]
    node, place = lax.axis_index("node"), lax.axis_index("local")
    tokens, half, mask = lax.optimization_barrier(
        (tokens, (node & (ratio - 1))[None], ((node >> (ratio.bit_length() - 1)) ^ place)[None])
    )
    chunk = rows // CHUNKS
    part = chunk // 2
    orders = (bits, bits[::-1])

    def permute(x, move):
        return lax.ppermute(x, AXES, pairs(move, places, ratio))

    def features_of(x, earlier):
        got = [permute(x, lambda p, h, q, j=j: (q ^ j, h, p)) for j in range(places)]

        def by_place(out_ref, i, value):
            out_ref[i] = value

        def by_half(out_ref, i, value):
            out_ref[:, :, i * feats : (i + 1) * feats] = value

        got = shuffle(got, mask, earlier, (places, rows, feats), by_place)
        halves = [got] + [permute(got, lambda p, h, q, e=e: (p, h ^ e, q)) for e in range(1, ratio)]
        return shuffle(halves, half, (), (places, rows, owned), by_half)

    def reduce_local(x, order):
        ks = list(range(places))
        x = x.astype(jnp.float32)
        for bit in order:
            away = [i for i, k in enumerate(ks) if k & bit]
            stay = [i for i, k in enumerate(ks) if not k & bit]
            sent = jnp.stack([x[:, i] for i in away], axis=1).astype(jnp.bfloat16)
            got = permute(sent, lambda p, h, q: (p, h, q ^ bit))
            x = jnp.stack([x[:, i] for i in stay], axis=1) + got.astype(jnp.float32)
            ks = [ks[i] for i in stay]
        return x[:, 0]

    def gather_local(x):
        direct = {bit: permute(x, lambda p, h, q: (p, h, q ^ bit)) for bit in bits}
        pieces, spots = [x] + [direct[bit] for bit in bits], [(0, 0)] + [(bit, 0) for bit in bits]
        for s, order in enumerate(orders):
            held = {0: None}
            for bit in order:
                for k in list(held):
                    if k == 0:
                        held[bit] = direct[bit][s : s + 1]
                    else:
                        held[k ^ bit] = permute(held[k], lambda p, h, q: (p, h, q ^ bit))
                        pieces.append(held[k ^ bit])
                        spots.append((k ^ bit, s * part))
        return pieces, spots

    w_gu, done = dequant(gate_up_codes, gate_up_scales)
    features = features_of(tokens, [done])
    hidden, pieces, spots = [], [], []
    for c in range(CHUNKS):
        flat = features[:, c * chunk : (c + 1) * chunk].reshape(places * chunk, owned)
        partial = [
            jnp.dot(flat, w_gu[g], preferred_element_type=jnp.float32)
            .astype(jnp.bfloat16)
            .reshape(places, chunk, group)
            for g in range(2)
        ]
        streams = []
        for s in range(2):
            at = slice(s * part, (s + 1) * part)
            both = reduce_local(jnp.stack([p[:, at] for p in partial]), orders[s])
            gate, up = both[0], both[1]
            sigmoid_gate = jax.nn.sigmoid(gate)
            active = gate * sigmoid_gate
            hidden.append((active * up).astype(jnp.bfloat16))
            first = c * chunk + s * part
            grad_in = d_hidden[first : first + part].astype(jnp.float32)
            d_gate = grad_in * up * sigmoid_gate * (1.0 + gate * (1.0 - sigmoid_gate))
            d_up = grad_in * active
            streams.append(jnp.stack([d_gate, d_up]).astype(jnp.bfloat16))
        blocks, places_of = gather_local(jnp.stack(streams))
        pieces += blocks
        spots += [k * rows + c * chunk + first for k, first in places_of]
    d_all, *term = input_grad(pieces, spots, w_gu, half, ratio, places * rows)
    summed = term[0].astype(jnp.float32)
    for e in range(1, ratio):
        got = permute(term[e], lambda p, h, q: (p, h ^ e, q))
        summed = summed + got.astype(jnp.float32)
    summed = summed.astype(jnp.bfloat16).reshape(places, rows, feats)
    arrived = [summed[0]] + [
        permute(summed[k], lambda p, h, q: (p, h, q ^ k)) for k in range(1, places)
    ]
    arrived = shuffle(arrived, mask)
    summands = [arrived[0]] + [
        permute(arrived[j], lambda p, h, q: (p ^ j, h, q)) for j in range(1, places)
    ]
    scale = 1.0 / math.sqrt(rows * places)
    turned = features.reshape(places * rows, owned).T
    grads, _ = weight_grad(0, turned, d_all, scale, summed[0, :16])
    grads, done = weight_grad(1, turned, d_all, scale, arrived[0][:16], grads)
    summands[0] = after(summands[0], done)
    d_tokens = sum(x.astype(jnp.float32) for x in summands).astype(jnp.bfloat16)
    return jnp.concatenate(hidden), d_tokens, grads


def solution(mesh):
    placed = (
        P("local", "node"),
        P(None, "local", "node"),
        P(None, "local", "node"),
        P("local", "node"),
    )
    return jax.shard_map(
        body,
        mesh=mesh,
        in_specs=placed,
        out_specs=(P("local", "node"), P("local", "node"), P(None, "local", "node")),
        check_vma=False,
    )
```

```python
import functools
import math

import jax
import jax.numpy as jnp
from jax import lax
from jax.experimental import pallas as pl
from jax.experimental.pallas import tpu as pltpu
from jax.sharding import PartitionSpec as P

BLOCK = 128
CHUNKS = 2
AXES = ("node", "local")


def in_vmem(x):
    return pltpu.with_memory_space_constraint(x, pltpu.VMEM)


def dequant_kernel(codes_ref, scales_ref, w_ref, done_ref):
    done_ref[0] = 0
    row = pl.ds(pl.program_id(0), 1)
    for g in range(2):
        w_ref[g] = (codes_ref[g].astype(jnp.float32) * scales_ref[g, row, :]).astype(jnp.bfloat16)


def dequant(codes, scales):
    _, owned, group = codes.shape
    blocks = owned // BLOCK
    return pl.pallas_call(
        dequant_kernel,
        grid=(blocks,),
        in_specs=[
            pl.BlockSpec((2, BLOCK, group), lambda i: (0, i, 0)),
            pl.BlockSpec((2, blocks, group), lambda i: (0, 0, 0)),
        ],
        out_specs=[
            pl.BlockSpec((2, BLOCK, group), lambda i: (0, i, 0)),
            pl.BlockSpec(memory_space=pltpu.SMEM),
        ],
        out_shape=[
            pltpu.VMEM(codes.shape, jnp.bfloat16),
            jax.ShapeDtypeStruct((1,), jnp.int32),
        ],
        compiler_params=pltpu.CompilerParams(vmem_limit_bytes=16 * 1024 * 1024),
    )(pltpu.with_memory_space_constraint(codes, pltpu.HBM), scales.astype(jnp.float32))


def pairs(move, places, ratio):
    out = []
    for plane in range(places):
        for half in range(ratio):
            for place in range(places):
                p, h, q = move(plane, half, place)
                out.append(
                    ((plane * ratio + half) * places + place, (p * ratio + h) * places + q)
                )
    return out


def after(x, earlier):
    return lax.optimization_barrier((x, earlier))[0]


def shuffle_kernel(count, write, index_ref, *refs):
    choices, outs = refs[:count], refs[-1:] if write else refs[-count:]
    for i in range(count):
        for j in range(count):

            @pl.when(index_ref[0] == i ^ j)
            def _():
                if write:
                    write(outs[0], i, choices[j][...])
                else:
                    outs[i][...] = choices[j][...]


def shuffle(choices, index, earlier=(), shape=None, write=None):
    one = choices[0]
    shapes = [shape] if write else [one.shape] * len(choices)
    out = pl.pallas_call(
        functools.partial(shuffle_kernel, len(choices), write),
        in_specs=[pl.BlockSpec(memory_space=pltpu.SMEM)]
        + [pl.BlockSpec(memory_space=pltpu.VMEM)] * len(choices)
        + [pl.BlockSpec(memory_space=pl.ANY)] * len(earlier),
        out_specs=[pl.BlockSpec(memory_space=pltpu.VMEM)] * len(shapes),
        out_shape=[pltpu.VMEM(s, one.dtype) for s in shapes],
        compiler_params=pltpu.CompilerParams(vmem_limit_bytes=16 * 1024 * 1024),
    )(index, *[in_vmem(x) for x in choices], *earlier)
    return out[0] if write else list(out)


def input_grad_kernel(spots, outs, first, rows, chunk, half_ref, *refs):
    pieces, w_ref = refs[: len(spots)], refs[len(spots)]
    d_ref, *term_refs = refs[len(refs) - outs - 1 : -1]
    mine_ref = refs[-1]
    for piece, (k, row) in zip(pieces, spots):
        streams, _, part, _ = piece.shape
        for s in range(streams):
            d_ref[:, pl.ds(k * rows + first + row + s * part, part), :] = piece[s]
            mine_ref[:, pl.ds(k * chunk + row + s * part, part), :] = piece[s]
    numbers = (((1,), (1,)), ((), ()))
    for e, term_ref in enumerate(term_refs):
        feats = term_ref.shape[1]
        at = pl.ds(pl.multiple_of((half_ref[0] ^ e) * feats, feats), feats)
        term = lax.dot_general(mine_ref[0], w_ref[0, at, :], numbers, preferred_element_type=jnp.float32)
        term += lax.dot_general(mine_ref[1], w_ref[1, at, :], numbers, preferred_element_type=jnp.float32)
        term = term.astype(jnp.bfloat16)
        for k in range(mine_ref.shape[1] // chunk):
            term_ref[pl.ds(k * rows + first, chunk), :] = term[k * chunk : (k + 1) * chunk]


def input_grad(pieces, spots, w_gu, half, ratio, first, rows, chunk, earlier, filled=()):
    _, owned, group = w_gu.shape
    feats = owned // ratio
    places = 1 + max(k for k, _ in spots)
    operands = [half, *[in_vmem(x) for x in pieces], in_vmem(w_gu), *earlier, *[in_vmem(x) for x in filled]]
    return pl.pallas_call(
        functools.partial(input_grad_kernel, spots, ratio + 1, first, rows, chunk),
        in_specs=[pl.BlockSpec(memory_space=pltpu.SMEM)]
        + [pl.BlockSpec(memory_space=pltpu.VMEM)] * (len(pieces) + 1)
        + [pl.BlockSpec(memory_space=pl.ANY)] * len(earlier)
        + [pl.BlockSpec(memory_space=pltpu.VMEM)] * len(filled),
        out_specs=[pl.BlockSpec(memory_space=pltpu.VMEM)] * (ratio + 1),
        out_shape=[pltpu.VMEM((2, places * rows, group), jnp.bfloat16)]
        + [pltpu.VMEM((places * rows, feats), jnp.bfloat16)] * ratio,
        scratch_shapes=[pltpu.VMEM((2, places * chunk, group), jnp.bfloat16)],
        input_output_aliases={len(operands) - len(filled) + i: i for i in range(len(filled))},
        compiler_params=pltpu.CompilerParams(vmem_limit_bytes=16 * 1024 * 1024),
    )(*operands)


def weight_grad_kernel(scale, features_ref, d_ref, *refs):
    out_ref, done_ref = refs[-2:]
    done_ref[0] = 0
    out_ref[0] = scale * lax.dot_general(
        features_ref[...], d_ref[0], (((0,), (0,)), ((), ())), preferred_element_type=jnp.float32
    )


def weight_grad(which, features, d_both, scale, earlier, grads=None):
    total, owned = features.shape
    group = d_both.shape[2]
    step = min(owned, 256)
    operands = [features, in_vmem(d_both), earlier] + ([] if grads is None else [grads])
    return pl.pallas_call(
        functools.partial(weight_grad_kernel, scale),
        grid=(owned // step,),
        in_specs=[
            pl.BlockSpec((total, step), lambda i: (0, i)),
            pl.BlockSpec((1, total, group), lambda i: (which, 0, 0)),
        ]
        + [pl.BlockSpec(memory_space=pl.ANY)] * (len(operands) - 2),
        out_specs=[
            pl.BlockSpec((1, step, group), lambda i: (which, i, 0)),
            pl.BlockSpec(memory_space=pltpu.SMEM),
        ],
        out_shape=[
            jax.ShapeDtypeStruct((2, owned, group), jnp.float32),
            jax.ShapeDtypeStruct((1,), jnp.int32),
        ],
        input_output_aliases={} if grads is None else {3: 0},
        compiler_params=pltpu.CompilerParams(vmem_limit_bytes=16 * 1024 * 1024),
    )(*operands)


def body(tokens, gate_up_codes, gate_up_scales, d_hidden):
    rows, feats = tokens.shape
    nodes, places = lax.axis_size("node"), lax.axis_size("local")
    ratio = nodes // places
    _, owned, group = gate_up_codes.shape
    bits = [1 << b for b in range(places.bit_length() - 1)]
    node, place = lax.axis_index("node"), lax.axis_index("local")
    tokens, half, mask = lax.optimization_barrier(
        (tokens, (node & (ratio - 1))[None], ((node >> (ratio.bit_length() - 1)) ^ place)[None])
    )
    chunk = rows // CHUNKS
    orders = (bits, bits[::-1])

    def permute(x, move):
        return lax.ppermute(x, AXES, pairs(move, places, ratio))

    def features_of(x, earlier):
        got = [permute(x, lambda p, h, q, j=j: (q ^ j, h, p)) for j in range(places)]

        def by_place(out_ref, i, value):
            out_ref[i] = value

        def by_half(out_ref, i, value):
            out_ref[:, :, i * feats : (i + 1) * feats] = value

        got = shuffle(got, mask, earlier, (places, rows, feats), by_place)
        halves = [got] + [permute(got, lambda p, h, q, e=e: (p, h ^ e, q)) for e in range(1, ratio)]
        return shuffle(halves, half, (), (places, rows, owned), by_half)

    def sent(x, order, step):
        ks = [k for k in range(places) if not any(k & bit for bit in order[:step])]
        bit = order[step]
        away = [i for i, k in enumerate(ks) if k & bit]
        stay = [i for i, k in enumerate(ks) if not k & bit]
        out = jnp.stack([x[:, i] for i in away], axis=1).astype(jnp.bfloat16)
        keep = jnp.stack([x[:, i] for i in stay], axis=1).astype(jnp.float32)
        return keep, permute(out, lambda p, h, q: (p, h, q ^ bit))

    def start_forward(c):
        part = chunk // 2
        flat = features[:, c * chunk : (c + 1) * chunk].reshape(places * chunk, owned)
        partial = [
            jnp.dot(flat, w_gu[g], preferred_element_type=jnp.float32)
            .astype(jnp.bfloat16)
            .reshape(places, chunk, group)
            for g in range(2)
        ]
        halves = [jnp.stack([p[:, s * part : (s + 1) * part] for p in partial]) for s in range(2)]
        return list(zip(*[sent(x, orders[s], 0) for s, x in enumerate(halves)]))

    def next_sums(keep, got, step):
        summed = [k + g.astype(jnp.float32) for k, g in zip(keep, got)]
        return list(zip(*[sent(x, orders[s], step) for s, x in enumerate(summed)]))

    def gradients(keep, got, first):
        hidden, streams = [], []
        for k, g in zip(keep, got):
            gate, up = (k + g.astype(jnp.float32))[:, 0]
            sigmoid_gate = jax.nn.sigmoid(gate)
            active = gate * sigmoid_gate
            hidden.append((active * up).astype(jnp.bfloat16))
            grad_in = d_hidden[first : first + gate.shape[0]].astype(jnp.float32)
            first += gate.shape[0]
            d_gate = grad_in * up * sigmoid_gate * (1.0 + gate * (1.0 - sigmoid_gate))
            d_up = grad_in * active
            streams.append(jnp.stack([d_gate, d_up]).astype(jnp.bfloat16))
        return hidden, jnp.stack(streams)

    def send_direct(x):
        return {bit: permute(x, lambda p, h, q: (p, h, q ^ bit)) for bit in bits}

    def forward_rest(x, direct):
        part = x.shape[2]
        pieces, spots = [x] + [direct[bit] for bit in bits], [(0, 0)] + [(bit, 0) for bit in bits]
        for s, order in enumerate(orders):
            held = {0: None}
            for bit in order:
                for k in list(held):
                    if k == 0:
                        held[bit] = direct[bit][s : s + 1]
                    else:
                        held[k ^ bit] = permute(held[k], lambda p, h, q: (p, h, q ^ bit))
                        pieces.append(held[k ^ bit])
                        spots.append((k ^ bit, s * part))
        return pieces, spots

    w_gu, done = dequant(gate_up_codes, gate_up_scales)
    features = features_of(tokens, [done])
    (keep_a, got_a), (keep_b, got_b) = start_forward(0), start_forward(1)
    for step in range(1, len(bits)):
        keep_a, got_a = next_sums(keep_a, got_a, step)
        keep_b, got_b = next_sums(keep_b, got_b, step)
    hidden_b, streams_b = gradients(keep_b, got_b, chunk)
    hidden_a, streams_a = gradients(keep_a, after(got_a, streams_b), 0)
    direct_a, direct_b = send_direct(streams_a), send_direct(streams_b)
    rest_a, rest_b = forward_rest(streams_a, direct_a), forward_rest(streams_b, direct_b)
    filled = input_grad(*rest_b, w_gu, half, ratio, chunk, rows, chunk, hidden_b)
    filled = input_grad(*rest_a, w_gu, half, ratio, 0, rows, chunk, hidden_a, filled)
    hidden = hidden_a + hidden_b
    d_all, *term = filled
    summed = term[0].astype(jnp.float32)
    for e in range(1, ratio):
        got = permute(term[e], lambda p, h, q: (p, h ^ e, q))
        summed = summed + got.astype(jnp.float32)
    summed = summed.astype(jnp.bfloat16).reshape(places, rows, feats)
    arrived = [summed[0]] + [
        permute(summed[k], lambda p, h, q: (p, h, q ^ k)) for k in range(1, places)
    ]
    flat = features.reshape(places * rows, owned)
    scale = 1.0 / math.sqrt(rows * places)
    grads, done = weight_grad(0, flat, d_all, scale, summed[0, :16])
    arrived = shuffle(arrived, mask, [done])
    summands = [arrived[0]] + [
        permute(arrived[j], lambda p, h, q: (p ^ j, h, q)) for j in range(1, places)
    ]
    grads, done = weight_grad(1, flat, d_all, scale, arrived[0][:16], grads)
    summands[0] = after(summands[0], done)
    d_tokens = sum(x.astype(jnp.float32) for x in summands).astype(jnp.bfloat16)
    return jnp.concatenate(hidden), d_tokens, grads


def solution(mesh):
    placed = (
        P("local", "node"),
        P(None, "local", "node"),
        P(None, "local", "node"),
        P("local", "node"),
    )
    return jax.shard_map(
        body,
        mesh=mesh,
        in_specs=placed,
        out_specs=(P("local", "node"), P("local", "node"), P(None, "local", "node")),
        check_vma=False,
    )
```

```python
import functools
import math

import jax
import jax.numpy as jnp
from jax import lax
from jax.experimental import pallas as pl
from jax.experimental.pallas import tpu as pltpu
from jax.sharding import PartitionSpec as P

BLOCK = 128
CHUNKS = 2
AXES = ("node", "local")


def in_vmem(x):
    return pltpu.with_memory_space_constraint(x, pltpu.VMEM)


def dequant_kernel(codes_ref, scales_ref, w_ref, done_ref):
    done_ref[0] = 0
    row = pl.ds(pl.program_id(0), 1)
    for g in range(2):
        w_ref[g] = (codes_ref[g].astype(jnp.float32) * scales_ref[g, row, :]).astype(jnp.bfloat16)


def dequant(codes, scales):
    _, owned, group = codes.shape
    blocks = owned // BLOCK
    return pl.pallas_call(
        dequant_kernel,
        grid=(blocks,),
        in_specs=[
            pl.BlockSpec((2, BLOCK, group), lambda i: (0, i, 0)),
            pl.BlockSpec((2, blocks, group), lambda i: (0, 0, 0)),
        ],
        out_specs=[
            pl.BlockSpec((2, BLOCK, group), lambda i: (0, i, 0)),
            pl.BlockSpec(memory_space=pltpu.SMEM),
        ],
        out_shape=[
            pltpu.VMEM(codes.shape, jnp.bfloat16),
            jax.ShapeDtypeStruct((1,), jnp.int32),
        ],
        compiler_params=pltpu.CompilerParams(vmem_limit_bytes=16 * 1024 * 1024),
    )(pltpu.with_memory_space_constraint(codes, pltpu.HBM), scales.astype(jnp.float32))


def pairs(move, places, ratio):
    out = []
    for plane in range(places):
        for half in range(ratio):
            for place in range(places):
                p, h, q = move(plane, half, place)
                out.append(
                    ((plane * ratio + half) * places + place, (p * ratio + h) * places + q)
                )
    return out


def after(x, earlier):
    return lax.optimization_barrier((x, earlier))[0]


def shuffle_kernel(order, write, index_ref, *refs):
    count = len(order)
    choices, outs = refs[:count], refs[-1:] if write else refs[-count:]
    for i in range(count):
        for j, choice in zip(order, choices):

            @pl.when(index_ref[0] == i ^ j)
            def _():
                if write:
                    write(outs[0], i, choice[...])
                else:
                    outs[i][...] = choice[...]


def shuffle(choices, index, earlier=(), shape=None, write=None):
    one = choices[0]
    shapes = [shape] if write else [one.shape] * len(choices)
    out = pl.pallas_call(
        functools.partial(shuffle_kernel, list(choices), write),
        in_specs=[pl.BlockSpec(memory_space=pltpu.SMEM)]
        + [pl.BlockSpec(memory_space=pltpu.VMEM)] * len(choices)
        + [pl.BlockSpec(memory_space=pl.ANY)] * len(earlier),
        out_specs=[pl.BlockSpec(memory_space=pltpu.VMEM)] * len(shapes),
        out_shape=[pltpu.VMEM(s, one.dtype) for s in shapes],
        compiler_params=pltpu.CompilerParams(vmem_limit_bytes=16 * 1024 * 1024),
    )(index, *[in_vmem(x) for x in choices.values()], *earlier)
    return out[0] if write else list(out)


def own_half_kernel(half_ref, x_ref, w_ref, out_ref):
    places, rows, feats = x_ref.shape
    at = pl.ds(pl.multiple_of(half_ref[0] * feats, feats), feats)
    flat = x_ref[...].reshape(places * rows, feats)
    for g in range(2):
        out_ref[g] = jnp.dot(flat, w_ref[g, at, :], preferred_element_type=jnp.float32).reshape(
            out_ref.shape[1:]
        )


def own_half(x, w_gu, half):
    places, rows, _ = x.shape
    return pl.pallas_call(
        own_half_kernel,
        in_specs=[pl.BlockSpec(memory_space=pltpu.SMEM)] + [pl.BlockSpec(memory_space=pltpu.VMEM)] * 2,
        out_specs=pl.BlockSpec(memory_space=pltpu.VMEM),
        out_shape=pltpu.VMEM((2, places, rows, w_gu.shape[2]), jnp.float32),
        compiler_params=pltpu.CompilerParams(vmem_limit_bytes=12 * 1024 * 1024),
    )(half, in_vmem(x), in_vmem(w_gu))


def other_halves_kernel(count, first, chunk, aways, half_ref, *refs):
    others, w_ref, sum_ref, outs = refs[:count], refs[count], refs[count + 1], refs[count + 2 :]
    places, _, feats = others[0].shape
    part = chunk // len(aways)
    rows = pl.ds(first, chunk)
    for g in range(2):
        total = sum_ref[g, :, rows, :].reshape(places * chunk, -1)
        for e, other_ref in enumerate(others, 1):
            at = pl.ds(pl.multiple_of((half_ref[0] ^ e) * feats, feats), feats)
            flat = other_ref[:, rows, :].reshape(places * chunk, feats)
            total += jnp.dot(flat, w_ref[g, at, :], preferred_element_type=jnp.float32)
        for s, away in enumerate(aways):
            counts = [0, 0]
            for k in range(places):
                block = total[k * chunk + s * part : k * chunk + (s + 1) * part]
                kind = 0 if k & away else 1
                out_ref = outs[2 * s + kind]
                out_ref[g, counts[kind]] = block.astype(out_ref.dtype)
                counts[kind] += 1


def other_halves(others, w_gu, own, half, first, chunk, aways):
    _, places, _, group = own.shape
    shape = (2, places // 2, chunk // len(aways), group)
    outs = pl.pallas_call(
        functools.partial(other_halves_kernel, len(others), first, chunk, aways),
        in_specs=[pl.BlockSpec(memory_space=pltpu.SMEM)]
        + [pl.BlockSpec(memory_space=pltpu.VMEM)] * (len(others) + 2),
        out_specs=[pl.BlockSpec(memory_space=pltpu.VMEM)] * (2 * len(aways)),
        out_shape=[pltpu.VMEM(shape, jnp.bfloat16), pltpu.VMEM(shape, jnp.float32)] * len(aways),
        compiler_params=pltpu.CompilerParams(vmem_limit_bytes=16 * 1024 * 1024),
    )(half, *[in_vmem(x) for x in others], in_vmem(w_gu), in_vmem(own))
    return outs[0::2], outs[1::2]


def input_grad_kernel(spots, outs, first, rows, chunk, half_ref, *refs):
    pieces, w_ref = refs[: len(spots)], refs[len(spots)]
    d_ref, *term_refs = refs[len(refs) - outs - 1 : -1]
    mine_ref = refs[-1]
    for piece, (k, row) in zip(pieces, spots):
        streams, _, part, _ = piece.shape
        for s in range(streams):
            d_ref[:, pl.ds(k * rows + first + row + s * part, part), :] = piece[s]
            mine_ref[:, pl.ds(k * chunk + row + s * part, part), :] = piece[s]
    numbers = (((1,), (1,)), ((), ()))
    for e, term_ref in enumerate(term_refs):
        feats = term_ref.shape[1]
        at = pl.ds(pl.multiple_of((half_ref[0] ^ e) * feats, feats), feats)
        term = lax.dot_general(mine_ref[0], w_ref[0, at, :], numbers, preferred_element_type=jnp.float32)
        term += lax.dot_general(mine_ref[1], w_ref[1, at, :], numbers, preferred_element_type=jnp.float32)
        term = term.astype(jnp.bfloat16)
        for k in range(mine_ref.shape[1] // chunk):
            term_ref[pl.ds(k * rows + first, chunk), :] = term[k * chunk : (k + 1) * chunk]


def input_grad(pieces, spots, w_gu, half, ratio, first, rows, chunk, earlier, filled=()):
    _, owned, group = w_gu.shape
    feats = owned // ratio
    places = 1 + max(k for k, _ in spots)
    operands = [half, *[in_vmem(x) for x in pieces], in_vmem(w_gu), *earlier, *[in_vmem(x) for x in filled]]
    return pl.pallas_call(
        functools.partial(input_grad_kernel, spots, ratio + 1, first, rows, chunk),
        in_specs=[pl.BlockSpec(memory_space=pltpu.SMEM)]
        + [pl.BlockSpec(memory_space=pltpu.VMEM)] * (len(pieces) + 1)
        + [pl.BlockSpec(memory_space=pl.ANY)] * len(earlier)
        + [pl.BlockSpec(memory_space=pltpu.VMEM)] * len(filled),
        out_specs=[pl.BlockSpec(memory_space=pltpu.VMEM)] * (ratio + 1),
        out_shape=[pltpu.VMEM((2, places * rows, group), jnp.bfloat16)]
        + [pltpu.VMEM((places * rows, feats), jnp.bfloat16)] * ratio,
        scratch_shapes=[pltpu.VMEM((2, places * chunk, group), jnp.bfloat16)],
        input_output_aliases={len(operands) - len(filled) + i: i for i in range(len(filled))},
        compiler_params=pltpu.CompilerParams(vmem_limit_bytes=16 * 1024 * 1024),
    )(*operands)


def weight_grad_kernel(scale, features_ref, d_ref, *refs):
    out_ref, done_ref = refs[-2:]
    done_ref[0] = 0
    out_ref[0] = scale * lax.dot_general(
        features_ref[...], d_ref[0], (((0,), (0,)), ((), ())), preferred_element_type=jnp.float32
    )


def weight_grad(which, features, d_both, scale, earlier, grads=None):
    total, owned = features.shape
    group = d_both.shape[2]
    step = min(owned, 256)
    operands = [features, in_vmem(d_both), earlier] + ([] if grads is None else [grads])
    return pl.pallas_call(
        functools.partial(weight_grad_kernel, scale),
        grid=(owned // step,),
        in_specs=[
            pl.BlockSpec((total, step), lambda i: (0, i)),
            pl.BlockSpec((1, total, group), lambda i: (which, 0, 0)),
        ]
        + [pl.BlockSpec(memory_space=pl.ANY)] * (len(operands) - 2),
        out_specs=[
            pl.BlockSpec((1, step, group), lambda i: (which, i, 0)),
            pl.BlockSpec(memory_space=pltpu.SMEM),
        ],
        out_shape=[
            jax.ShapeDtypeStruct((2, owned, group), jnp.float32),
            jax.ShapeDtypeStruct((1,), jnp.int32),
        ],
        input_output_aliases={} if grads is None else {3: 0},
        compiler_params=pltpu.CompilerParams(vmem_limit_bytes=16 * 1024 * 1024),
    )(*operands)


def body(tokens, gate_up_codes, gate_up_scales, d_hidden):
    rows, feats = tokens.shape
    nodes, places = lax.axis_size("node"), lax.axis_size("local")
    ratio = nodes // places
    _, owned, group = gate_up_codes.shape
    bits = [1 << b for b in range(places.bit_length() - 1)]
    node, place = lax.axis_index("node"), lax.axis_index("local")
    tokens, half, mask = lax.optimization_barrier(
        (tokens, (node & (ratio - 1))[None], ((node >> (ratio.bit_length() - 1)) ^ place)[None])
    )
    chunk = rows // CHUNKS
    part = chunk // 2
    orders = (bits, bits[::-1])

    def permute(x, move):
        return lax.ppermute(x, AXES, pairs(move, places, ratio))

    def own_features(x, earlier):
        got = {j: permute(x, lambda p, h, q: (q ^ j, h, p)) for j in [*range(1, places), 0]}

        def by_place(out_ref, i, value):
            out_ref[i] = value

        return shuffle(got, mask, earlier, (places, rows, feats), by_place)

    def joined(halves):
        def by_half(out_ref, i, value):
            out_ref[:, :, i * feats : (i + 1) * feats] = value

        return shuffle(dict(enumerate(halves)), half, (), (places, rows, owned), by_half)

    def sent(x, order, step):
        ks = [k for k in range(places) if not any(k & bit for bit in order[:step])]
        bit = order[step]
        away = [i for i, k in enumerate(ks) if k & bit]
        stay = [i for i, k in enumerate(ks) if not k & bit]
        out = jnp.stack([x[:, i] for i in away], axis=1).astype(jnp.bfloat16)
        keep = jnp.stack([x[:, i] for i in stay], axis=1).astype(jnp.float32)
        return keep, permute(out, lambda p, h, q: (p, h, q ^ bit))

    def start_forward(c):
        aways = [order[0] for order in orders]
        out, keep = other_halves(others, w_gu, own, half, c * chunk, chunk, aways)
        return keep, [
            permute(x, lambda p, h, q, bit=bit: (p, h, q ^ bit)) for x, bit in zip(out, aways)
        ]

    def next_sums(keep, got, step):
        summed = [k + g.astype(jnp.float32) for k, g in zip(keep, got)]
        return list(zip(*[sent(x, orders[s], step) for s, x in enumerate(summed)]))

    def gradients(keep, got, first):
        hidden, streams = [], []
        for k, g in zip(keep, got):
            gate, up = (k + g.astype(jnp.float32))[:, 0]
            sigmoid_gate = jax.nn.sigmoid(gate)
            active = gate * sigmoid_gate
            hidden.append((active * up).astype(jnp.bfloat16))
            grad_in = d_hidden[first : first + gate.shape[0]].astype(jnp.float32)
            first += gate.shape[0]
            d_gate = grad_in * up * sigmoid_gate * (1.0 + gate * (1.0 - sigmoid_gate))
            d_up = grad_in * active
            streams.append(jnp.stack([d_gate, d_up]).astype(jnp.bfloat16))
        return hidden, jnp.stack(streams)

    def send_direct(x):
        return {bit: permute(x, lambda p, h, q: (p, h, q ^ bit)) for bit in bits}

    def forward_rest(x, direct):
        part = x.shape[2]
        pieces, spots = [x] + [direct[bit] for bit in bits], [(0, 0)] + [(bit, 0) for bit in bits]
        for s, order in enumerate(orders):
            held = {0: None}
            for bit in order:
                for k in list(held):
                    if k == 0:
                        held[bit] = direct[bit][s : s + 1]
                    else:
                        held[k ^ bit] = permute(held[k], lambda p, h, q: (p, h, q ^ bit))
                        pieces.append(held[k ^ bit])
                        spots.append((k ^ bit, s * part))
        return pieces, spots

    w_gu, done = dequant(gate_up_codes, gate_up_scales)
    mine = own_features(tokens, [done])
    others = [permute(mine, lambda p, h, q, e=e: (p, h ^ e, q)) for e in range(1, ratio)]
    own = own_half(mine, w_gu, half)
    (keep_a, got_a), (keep_b, got_b) = start_forward(0), start_forward(1)
    for step in range(1, len(bits)):
        keep_a, got_a = next_sums(keep_a, got_a, step)
        keep_b, got_b = next_sums(keep_b, got_b, step)
    hidden_b, streams_b = gradients(keep_b, got_b, chunk)
    hidden_a, streams_a = gradients(keep_a, after(got_a, streams_b), 0)
    direct_a, direct_b = send_direct(streams_a), send_direct(streams_b)
    rest_a, rest_b = forward_rest(streams_a, direct_a), forward_rest(streams_b, direct_b)
    filled = input_grad(*rest_b, w_gu, half, ratio, chunk, rows, chunk, hidden_b)
    filled = input_grad(*rest_a, w_gu, half, ratio, 0, rows, chunk, hidden_a, filled)
    d_all, *term = filled
    summed = term[0].astype(jnp.float32)
    for e in range(1, ratio):
        got = permute(term[e], lambda p, h, q: (p, h ^ e, q))
        summed = summed + got.astype(jnp.float32)
    summed = summed.astype(jnp.bfloat16).reshape(places, rows, feats)
    arrived = [summed[0]] + [
        permute(summed[k], lambda p, h, q: (p, h, q ^ k)) for k in range(1, places)
    ]
    flat = joined([mine] + others).reshape(places * rows, owned)
    scale = 1.0 / math.sqrt(rows * places)
    grads, done = weight_grad(0, flat, d_all, scale, summed[0, :16])
    arrived = shuffle(dict(enumerate(arrived)), mask, [done])
    summands = [arrived[0]] + [
        permute(arrived[j], lambda p, h, q: (p ^ j, h, q)) for j in range(1, places)
    ]
    grads, done = weight_grad(1, flat, d_all, scale, arrived[0][:16], grads)
    summands[0] = after(summands[0], done)
    d_tokens = sum(x.astype(jnp.float32) for x in summands).astype(jnp.bfloat16)
    return jnp.concatenate(hidden_a + hidden_b), d_tokens, grads


def solution(mesh):
    placed = (
        P("local", "node"),
        P(None, "local", "node"),
        P(None, "local", "node"),
        P("local", "node"),
    )
    return jax.shard_map(
        body,
        mesh=mesh,
        in_specs=placed,
        out_specs=(P("local", "node"), P("local", "node"), P(None, "local", "node")),
        check_vma=False,
    )
```

```python
import functools
import math

import jax
import jax.numpy as jnp
from jax import lax
from jax.experimental import pallas as pl
from jax.experimental.pallas import tpu as pltpu
from jax.sharding import PartitionSpec as P

BLOCK = 128
CHUNKS = 2
AXES = ("node", "local")


def in_vmem(x):
    return pltpu.with_memory_space_constraint(x, pltpu.VMEM)


def dequant_kernel(codes_ref, scales_ref, w_ref, done_ref, narrow_ref, wide_ref, sem, scales_sem):
    done_ref[0] = 0
    _, owned, group = w_ref.shape
    tile = 16

    def copy(b):
        at = pl.ds(b * BLOCK, BLOCK)
        return pltpu.make_async_copy(codes_ref.at[:, at, :], w_ref.at[:, at, :], sem.at[b])

    scales = pltpu.make_async_copy(scales_ref, narrow_ref, scales_sem)
    scales.start()
    for b in range(owned // BLOCK):
        copy(b).start()
    scales.wait()
    wide_ref[...] = narrow_ref[...].astype(jnp.float32)
    for b in range(owned // BLOCK):
        copy(b).wait()
        for g in range(2):
            scale = jnp.broadcast_to(wide_ref[g, b : b + 1, :], (tile, group)).astype(jnp.bfloat16)
            for t in range(b * BLOCK, (b + 1) * BLOCK, tile):
                w_ref[g, t : t + tile] = w_ref[g, t : t + tile] * scale


def dequant(codes, scales):
    codes, scales = (pltpu.with_memory_space_constraint(x, pltpu.HBM) for x in (codes, scales))
    return pl.pallas_call(
        dequant_kernel,
        in_specs=[pl.BlockSpec(memory_space=pl.ANY)] * 2,
        out_specs=[pl.BlockSpec(memory_space=pltpu.VMEM), pl.BlockSpec(memory_space=pltpu.SMEM)],
        out_shape=[
            pltpu.VMEM(codes.shape, jnp.bfloat16),
            jax.ShapeDtypeStruct((1,), jnp.int32),
        ],
        scratch_shapes=[
            pltpu.VMEM(scales.shape, jnp.bfloat16),
            pltpu.VMEM(scales.shape, jnp.float32),
            pltpu.SemaphoreType.DMA((codes.shape[1] // BLOCK,)),
            pltpu.SemaphoreType.DMA,
        ],
        compiler_params=pltpu.CompilerParams(vmem_limit_bytes=12 * 1024 * 1024),
    )(codes, scales)


def pairs(move, places, ratio):
    out = []
    for plane in range(places):
        for half in range(ratio):
            for place in range(places):
                p, h, q = move(plane, half, place)
                out.append(
                    ((plane * ratio + half) * places + place, (p * ratio + h) * places + q)
                )
    return out


def after(x, earlier):
    return lax.optimization_barrier((x, earlier))[0]


def shuffle_kernel(order, write, index_ref, *refs):
    count = len(order)
    choices, outs = refs[:count], refs[-1:] if write else refs[-count:]
    for i in range(count):
        for j, choice in zip(order, choices):

            @pl.when(index_ref[0] == i ^ j)
            def _():
                if write:
                    write(outs[0], i, choice[...])
                else:
                    outs[i][...] = choice[...]


def shuffle(choices, index, earlier=(), shape=None, write=None):
    one = choices[0]
    shapes = [shape] if write else [one.shape] * len(choices)
    out = pl.pallas_call(
        functools.partial(shuffle_kernel, list(choices), write),
        in_specs=[pl.BlockSpec(memory_space=pltpu.SMEM)]
        + [pl.BlockSpec(memory_space=pltpu.VMEM)] * len(choices)
        + [pl.BlockSpec(memory_space=pl.ANY)] * len(earlier),
        out_specs=[pl.BlockSpec(memory_space=pltpu.VMEM)] * len(shapes),
        out_shape=[pltpu.VMEM(s, one.dtype) for s in shapes],
        compiler_params=pltpu.CompilerParams(vmem_limit_bytes=16 * 1024 * 1024),
    )(index, *[in_vmem(x) for x in choices.values()], *earlier)
    return out[0] if write else list(out)


def own_half_kernel(half_ref, x_ref, w_ref, out_ref):
    places, rows, feats = x_ref.shape
    at = pl.ds(pl.multiple_of(half_ref[0] * feats, feats), feats)
    flat = x_ref[...].reshape(places * rows, feats)
    for g in range(2):
        out_ref[g] = jnp.dot(flat, w_ref[g, at, :], preferred_element_type=jnp.float32).reshape(
            out_ref.shape[1:]
        )


def own_half(x, w_gu, half):
    places, rows, _ = x.shape
    return pl.pallas_call(
        own_half_kernel,
        in_specs=[pl.BlockSpec(memory_space=pltpu.SMEM)] + [pl.BlockSpec(memory_space=pltpu.VMEM)] * 2,
        out_specs=pl.BlockSpec(memory_space=pltpu.VMEM),
        out_shape=pltpu.VMEM((2, places, rows, w_gu.shape[2]), jnp.float32),
        compiler_params=pltpu.CompilerParams(vmem_limit_bytes=12 * 1024 * 1024),
    )(half, in_vmem(x), in_vmem(w_gu))


def other_halves_kernel(count, first, chunk, aways, half_ref, *refs):
    others, w_ref, sum_ref, outs = refs[:count], refs[count], refs[count + 1], refs[count + 2 :]
    places, _, feats = others[0].shape
    part = chunk // len(aways)
    rows = pl.ds(first, chunk)
    for g in range(2):
        total = sum_ref[g, :, rows, :].reshape(places * chunk, -1)
        for e, other_ref in enumerate(others, 1):
            at = pl.ds(pl.multiple_of((half_ref[0] ^ e) * feats, feats), feats)
            flat = other_ref[:, rows, :].reshape(places * chunk, feats)
            total += jnp.dot(flat, w_ref[g, at, :], preferred_element_type=jnp.float32)
        for s, away in enumerate(aways):
            counts = [0, 0]
            for k in range(places):
                block = total[k * chunk + s * part : k * chunk + (s + 1) * part]
                kind = 0 if k & away else 1
                out_ref = outs[2 * s + kind]
                out_ref[g, counts[kind]] = block.astype(out_ref.dtype)
                counts[kind] += 1


def other_halves(others, w_gu, own, half, first, chunk, aways):
    _, places, _, group = own.shape
    shape = (2, places // 2, chunk // len(aways), group)
    outs = pl.pallas_call(
        functools.partial(other_halves_kernel, len(others), first, chunk, aways),
        in_specs=[pl.BlockSpec(memory_space=pltpu.SMEM)]
        + [pl.BlockSpec(memory_space=pltpu.VMEM)] * (len(others) + 2),
        out_specs=[pl.BlockSpec(memory_space=pltpu.VMEM)] * (2 * len(aways)),
        out_shape=[pltpu.VMEM(shape, jnp.bfloat16), pltpu.VMEM(shape, jnp.float32)] * len(aways),
        compiler_params=pltpu.CompilerParams(vmem_limit_bytes=16 * 1024 * 1024),
    )(half, *[in_vmem(x) for x in others], in_vmem(w_gu), in_vmem(own))
    return outs[0::2], outs[1::2]


def input_grad_kernel(spots, outs, first, rows, chunk, half_ref, *refs):
    pieces, w_ref = refs[: len(spots)], refs[len(spots)]
    d_ref, *term_refs = refs[len(refs) - outs - 1 : -1]
    mine_ref = refs[-1]
    for piece, (k, row) in zip(pieces, spots):
        streams, _, part, _ = piece.shape
        for s in range(streams):
            d_ref[:, pl.ds(k * rows + first + row + s * part, part), :] = piece[s]
            mine_ref[:, pl.ds(k * chunk + row + s * part, part), :] = piece[s]
    numbers = (((1,), (1,)), ((), ()))
    for e, term_ref in enumerate(term_refs):
        feats = term_ref.shape[1]
        at = pl.ds(pl.multiple_of((half_ref[0] ^ e) * feats, feats), feats)
        term = lax.dot_general(mine_ref[0], w_ref[0, at, :], numbers, preferred_element_type=jnp.float32)
        term += lax.dot_general(mine_ref[1], w_ref[1, at, :], numbers, preferred_element_type=jnp.float32)
        term = term.astype(jnp.bfloat16)
        for k in range(mine_ref.shape[1] // chunk):
            term_ref[pl.ds(k * rows + first, chunk), :] = term[k * chunk : (k + 1) * chunk]


def input_grad(pieces, spots, w_gu, half, ratio, first, rows, chunk, earlier, filled=()):
    _, owned, group = w_gu.shape
    feats = owned // ratio
    places = 1 + max(k for k, _ in spots)
    operands = [half, *[in_vmem(x) for x in pieces], in_vmem(w_gu), *earlier, *[in_vmem(x) for x in filled]]
    return pl.pallas_call(
        functools.partial(input_grad_kernel, spots, ratio + 1, first, rows, chunk),
        in_specs=[pl.BlockSpec(memory_space=pltpu.SMEM)]
        + [pl.BlockSpec(memory_space=pltpu.VMEM)] * (len(pieces) + 1)
        + [pl.BlockSpec(memory_space=pl.ANY)] * len(earlier)
        + [pl.BlockSpec(memory_space=pltpu.VMEM)] * len(filled),
        out_specs=[pl.BlockSpec(memory_space=pltpu.VMEM)] * (ratio + 1),
        out_shape=[pltpu.VMEM((2, places * rows, group), jnp.bfloat16)]
        + [pltpu.VMEM((places * rows, feats), jnp.bfloat16)] * ratio,
        scratch_shapes=[pltpu.VMEM((2, places * chunk, group), jnp.bfloat16)],
        input_output_aliases={len(operands) - len(filled) + i: i for i in range(len(filled))},
        compiler_params=pltpu.CompilerParams(vmem_limit_bytes=16 * 1024 * 1024),
    )(*operands)


def weight_grad_kernel(scale, features_ref, d_ref, *refs):
    out_ref, done_ref = refs[-2:]
    done_ref[0] = 0
    out_ref[0] = scale * lax.dot_general(
        features_ref[...], d_ref[0], (((0,), (0,)), ((), ())), preferred_element_type=jnp.float32
    )


def weight_grad(which, features, d_both, scale, earlier, grads=None):
    total, owned = features.shape
    group = d_both.shape[2]
    step = min(owned, 256)
    operands = [features, in_vmem(d_both), earlier] + ([] if grads is None else [grads])
    return pl.pallas_call(
        functools.partial(weight_grad_kernel, scale),
        grid=(owned // step,),
        in_specs=[
            pl.BlockSpec((total, step), lambda i: (0, i)),
            pl.BlockSpec((1, total, group), lambda i: (which, 0, 0)),
        ]
        + [pl.BlockSpec(memory_space=pl.ANY)] * (len(operands) - 2),
        out_specs=[
            pl.BlockSpec((1, step, group), lambda i: (which, i, 0)),
            pl.BlockSpec(memory_space=pltpu.SMEM),
        ],
        out_shape=[
            jax.ShapeDtypeStruct((2, owned, group), jnp.float32),
            jax.ShapeDtypeStruct((1,), jnp.int32),
        ],
        input_output_aliases={} if grads is None else {3: 0},
        compiler_params=pltpu.CompilerParams(vmem_limit_bytes=16 * 1024 * 1024),
    )(*operands)


def body(tokens, gate_up_codes, gate_up_scales, d_hidden):
    rows, feats = tokens.shape
    nodes, places = lax.axis_size("node"), lax.axis_size("local")
    ratio = nodes // places
    _, owned, group = gate_up_codes.shape
    bits = [1 << b for b in range(places.bit_length() - 1)]
    node, place = lax.axis_index("node"), lax.axis_index("local")
    tokens, half, mask = lax.optimization_barrier(
        (tokens, (node & (ratio - 1))[None], ((node >> (ratio.bit_length() - 1)) ^ place)[None])
    )
    chunk = rows // CHUNKS
    part = chunk // 2
    orders = (bits, bits[::-1])

    def permute(x, move):
        return lax.ppermute(x, AXES, pairs(move, places, ratio))

    def own_features(x, earlier):
        got = {j: permute(x, lambda p, h, q: (q ^ j, h, p)) for j in [*range(1, places), 0]}

        def by_place(out_ref, i, value):
            out_ref[i] = value

        return shuffle(got, mask, earlier, (places, rows, feats), by_place)

    def joined(halves):
        def by_half(out_ref, i, value):
            out_ref[:, :, i * feats : (i + 1) * feats] = value

        return shuffle(dict(enumerate(halves)), half, (), (places, rows, owned), by_half)

    def sent(x, order, step):
        ks = [k for k in range(places) if not any(k & bit for bit in order[:step])]
        bit = order[step]
        away = [i for i, k in enumerate(ks) if k & bit]
        stay = [i for i, k in enumerate(ks) if not k & bit]
        out = jnp.stack([x[:, i] for i in away], axis=1).astype(jnp.bfloat16)
        keep = jnp.stack([x[:, i] for i in stay], axis=1).astype(jnp.float32)
        return keep, permute(out, lambda p, h, q: (p, h, q ^ bit))

    def start_forward(c):
        aways = [order[0] for order in orders]
        out, keep = other_halves(others, w_gu, own, half, c * chunk, chunk, aways)
        return keep, [
            permute(x, lambda p, h, q, bit=bit: (p, h, q ^ bit)) for x, bit in zip(out, aways)
        ]

    def next_sums(keep, got, step):
        summed = [k + g.astype(jnp.float32) for k, g in zip(keep, got)]
        return list(zip(*[sent(x, orders[s], step) for s, x in enumerate(summed)]))

    def gradients(keep, got, first):
        hidden, streams = [], []
        for k, g in zip(keep, got):
            gate, up = (k + g.astype(jnp.float32))[:, 0]
            sigmoid_gate = jax.nn.sigmoid(gate)
            active = gate * sigmoid_gate
            hidden.append((active * up).astype(jnp.bfloat16))
            grad_in = d_hidden[first : first + gate.shape[0]].astype(jnp.float32)
            first += gate.shape[0]
            d_gate = grad_in * up * sigmoid_gate * (1.0 + gate * (1.0 - sigmoid_gate))
            d_up = grad_in * active
            streams.append(jnp.stack([d_gate, d_up]).astype(jnp.bfloat16))
        return hidden, jnp.stack(streams)

    def send_direct(x):
        return {bit: permute(x, lambda p, h, q: (p, h, q ^ bit)) for bit in bits}

    def forward_rest(x, direct):
        part = x.shape[2]
        pieces, spots = [x] + [direct[bit] for bit in bits], [(0, 0)] + [(bit, 0) for bit in bits]
        for s, order in enumerate(orders):
            held = {0: None}
            for bit in order:
                for k in list(held):
                    if k == 0:
                        held[bit] = direct[bit][s : s + 1]
                    else:
                        held[k ^ bit] = permute(held[k], lambda p, h, q: (p, h, q ^ bit))
                        pieces.append(held[k ^ bit])
                        spots.append((k ^ bit, s * part))
        return pieces, spots

    w_gu, done = dequant(gate_up_codes, gate_up_scales)
    mine = own_features(tokens, [done])
    others = [permute(mine, lambda p, h, q, e=e: (p, h ^ e, q)) for e in range(1, ratio)]
    own = own_half(mine, w_gu, half)
    (keep_a, got_a), (keep_b, got_b) = start_forward(0), start_forward(1)
    for step in range(1, len(bits)):
        keep_a, got_a = next_sums(keep_a, got_a, step)
        keep_b, got_b = next_sums(keep_b, got_b, step)
    hidden_b, streams_b = gradients(keep_b, got_b, chunk)
    hidden_a, streams_a = gradients(keep_a, after(got_a, streams_b), 0)
    direct_a, direct_b = send_direct(streams_a), send_direct(streams_b)
    rest_a, rest_b = forward_rest(streams_a, direct_a), forward_rest(streams_b, direct_b)
    filled = input_grad(*rest_b, w_gu, half, ratio, chunk, rows, chunk, hidden_b)
    filled = input_grad(*rest_a, w_gu, half, ratio, 0, rows, chunk, hidden_a, filled)
    d_all, *term = filled
    summed = term[0].astype(jnp.float32)
    for e in range(1, ratio):
        got = permute(term[e], lambda p, h, q: (p, h ^ e, q))
        summed = summed + got.astype(jnp.float32)
    summed = summed.astype(jnp.bfloat16).reshape(places, rows, feats)
    far_first = [*range(places // 2, places), *range(1, places // 2)]
    arrived = {k: permute(summed[k], lambda p, h, q: (p, h, q ^ k)) for k in range(1, places)}
    arrived[0] = summed[0]
    flat = joined([mine] + others).reshape(places * rows, owned)
    scale = 1.0 / math.sqrt(rows * places)
    grads, done = weight_grad(0, flat, d_all, scale, summed[0, :16])
    arrived = shuffle(arrived, mask, [done])
    summands = [arrived[0]] + [
        permute(arrived[j], lambda p, h, q: (p ^ j, h, q)) for j in reversed(far_first)
    ]
    grads, done = weight_grad(1, flat, d_all, scale, arrived[0][:16], grads)
    summands[0] = after(summands[0], done)
    d_tokens = sum(x.astype(jnp.float32) for x in summands).astype(jnp.bfloat16)
    return jnp.concatenate(hidden_a + hidden_b), d_tokens, grads


def solution(mesh):
    placed = (
        P("local", "node"),
        P(None, "local", "node"),
        P(None, "local", "node"),
        P("local", "node"),
    )
    return jax.shard_map(
        body,
        mesh=mesh,
        in_specs=placed,
        out_specs=(P("local", "node"), P("local", "node"), P(None, "local", "node")),
        check_vma=False,
    )
```

```python
import functools
import math

import jax
import jax.numpy as jnp
from jax import lax
from jax.experimental import pallas as pl
from jax.experimental.pallas import tpu as pltpu
from jax.sharding import PartitionSpec as P

BLOCK = 128
CHUNKS = 2
AXES = ("node", "local")


def in_vmem(x):
    return pltpu.with_memory_space_constraint(x, pltpu.VMEM)


def mark(marks_ref, mask_ref):
    for i in range(marks_ref.shape[0]):
        marks_ref[i : i + 1, :] = jnp.where(mask_ref[0] == i, 1.0, 0.0) * jnp.ones_like(marks_ref[:1, :])


def pick(choices, i, marks):
    out = choices[i]
    for m in reversed(range(1, len(choices))):
        out = jnp.where(marks[m : m + 1] > 0.5, choices[i ^ m], out)
    return out


def dequant_kernel(mask_ref, codes_ref, scales_ref, w_ref, marks_ref, narrow_ref, wide_ref, sem, scales_sem):
    mark(marks_ref, mask_ref)
    _, owned, group = w_ref.shape
    tile = 16

    def copy(b):
        at = pl.ds(b * BLOCK, BLOCK)
        return pltpu.make_async_copy(codes_ref.at[:, at, :], w_ref.at[:, at, :], sem.at[b])

    scales = pltpu.make_async_copy(scales_ref, narrow_ref, scales_sem)
    scales.start()
    for b in range(owned // BLOCK):
        copy(b).start()
    scales.wait()
    wide_ref[...] = narrow_ref[...].astype(jnp.float32)
    for b in range(owned // BLOCK):
        copy(b).wait()
        for g in range(2):
            scale = jnp.broadcast_to(wide_ref[g, b : b + 1, :], (tile, group)).astype(jnp.bfloat16)
            for t in range(b * BLOCK, (b + 1) * BLOCK, tile):
                w_ref[g, t : t + tile] = w_ref[g, t : t + tile] * scale


def dequant(codes, scales, mask, marks_shape):
    codes, scales = (pltpu.with_memory_space_constraint(x, pltpu.HBM) for x in (codes, scales))
    return pl.pallas_call(
        dequant_kernel,
        in_specs=[pl.BlockSpec(memory_space=pltpu.SMEM)] + [pl.BlockSpec(memory_space=pl.ANY)] * 2,
        out_specs=[pl.BlockSpec(memory_space=pltpu.VMEM)] * 2,
        out_shape=[
            pltpu.VMEM(codes.shape, jnp.bfloat16),
            pltpu.VMEM(marks_shape, jnp.float32),
        ],
        scratch_shapes=[
            pltpu.VMEM(scales.shape, jnp.bfloat16),
            pltpu.VMEM(scales.shape, jnp.float32),
            pltpu.SemaphoreType.DMA((codes.shape[1] // BLOCK,)),
            pltpu.SemaphoreType.DMA,
        ],
        compiler_params=pltpu.CompilerParams(vmem_limit_bytes=12 * 1024 * 1024),
    )(mask, codes, scales)


def pairs(move, places, ratio):
    out = []
    for plane in range(places):
        for half in range(ratio):
            for place in range(places):
                p, h, q = move(plane, half, place)
                out.append(
                    ((plane * ratio + half) * places + place, (p * ratio + h) * places + q)
                )
    return out


def after(x, earlier):
    return lax.optimization_barrier((x, earlier))[0]


def shuffle_kernel(order, write, index_ref, *refs):
    count = len(order)
    choices, outs = refs[:count], refs[-1:] if write else refs[-count:]
    for i in range(count):
        for j, choice in zip(order, choices):

            @pl.when(index_ref[0] == i ^ j)
            def _():
                if write:
                    write(outs[0], i, choice[...])
                else:
                    outs[i][...] = choice[...]


def shuffle(choices, index, earlier=(), shape=None, write=None):
    one = choices[0]
    shapes = [shape] if write else [one.shape] * len(choices)
    out = pl.pallas_call(
        functools.partial(shuffle_kernel, list(choices), write),
        in_specs=[pl.BlockSpec(memory_space=pltpu.SMEM)]
        + [pl.BlockSpec(memory_space=pltpu.VMEM)] * len(choices)
        + [pl.BlockSpec(memory_space=pl.ANY)] * len(earlier),
        out_specs=[pl.BlockSpec(memory_space=pltpu.VMEM)] * len(shapes),
        out_shape=[pltpu.VMEM(s, one.dtype) for s in shapes],
        compiler_params=pltpu.CompilerParams(vmem_limit_bytes=16 * 1024 * 1024),
    )(index, *[in_vmem(x) for x in choices.values()], *earlier)
    return out[0] if write else list(out)


def own_half_kernel(half_ref, x_ref, w_ref, out_ref):
    places, rows, feats = x_ref.shape
    at = pl.ds(pl.multiple_of(half_ref[0] * feats, feats), feats)
    flat = x_ref[...].reshape(places * rows, feats)
    for g in range(2):
        out_ref[g] = jnp.dot(flat, w_ref[g, at, :], preferred_element_type=jnp.float32).reshape(
            out_ref.shape[1:]
        )


def own_half(x, w_gu, half):
    places, rows, _ = x.shape
    return pl.pallas_call(
        own_half_kernel,
        in_specs=[pl.BlockSpec(memory_space=pltpu.SMEM)] + [pl.BlockSpec(memory_space=pltpu.VMEM)] * 2,
        out_specs=pl.BlockSpec(memory_space=pltpu.VMEM),
        out_shape=pltpu.VMEM((2, places, rows, w_gu.shape[2]), jnp.float32),
        compiler_params=pltpu.CompilerParams(vmem_limit_bytes=12 * 1024 * 1024),
    )(half, in_vmem(x), in_vmem(w_gu))


def other_halves_kernel(count, first, chunk, aways, half_ref, *refs):
    others, w_ref, sum_ref, outs = refs[:count], refs[count], refs[count + 1], refs[count + 2 :]
    places, _, feats = others[0].shape
    part = chunk // len(aways)
    rows = pl.ds(first, chunk)
    for g in range(2):
        total = sum_ref[g, :, rows, :].reshape(places * chunk, -1)
        for e, other_ref in enumerate(others, 1):
            at = pl.ds(pl.multiple_of((half_ref[0] ^ e) * feats, feats), feats)
            flat = other_ref[:, rows, :].reshape(places * chunk, feats)
            total += jnp.dot(flat, w_ref[g, at, :], preferred_element_type=jnp.float32)
        for s, away in enumerate(aways):
            counts = [0, 0]
            for k in range(places):
                block = total[k * chunk + s * part : k * chunk + (s + 1) * part]
                kind = 0 if k & away else 1
                out_ref = outs[2 * s + kind]
                out_ref[g, counts[kind]] = block.astype(out_ref.dtype)
                counts[kind] += 1


def other_halves(others, w_gu, own, half, first, chunk, aways):
    _, places, _, group = own.shape
    shape = (2, places // 2, chunk // len(aways), group)
    outs = pl.pallas_call(
        functools.partial(other_halves_kernel, len(others), first, chunk, aways),
        in_specs=[pl.BlockSpec(memory_space=pltpu.SMEM)]
        + [pl.BlockSpec(memory_space=pltpu.VMEM)] * (len(others) + 2),
        out_specs=[pl.BlockSpec(memory_space=pltpu.VMEM)] * (2 * len(aways)),
        out_shape=[pltpu.VMEM(shape, jnp.bfloat16), pltpu.VMEM(shape, jnp.float32)] * len(aways),
        compiler_params=pltpu.CompilerParams(vmem_limit_bytes=16 * 1024 * 1024),
    )(half, *[in_vmem(x) for x in others], in_vmem(w_gu), in_vmem(own))
    return outs[0::2], outs[1::2]


def input_grad_kernel(spots, outs, first, count, half_ref, *refs):
    pieces, w_ref = refs[: len(spots)], refs[len(spots)]
    d_ref, *term_refs = refs[len(refs) - outs :]
    for piece, row in zip(pieces, spots):
        streams, _, part, _ = piece.shape
        for s in range(streams):
            d_ref[:, pl.ds(row + s * part, part), :] = piece[s]
    mine = pl.ds(first, count)
    numbers = (((1,), (1,)), ((), ()))
    for e, term_ref in enumerate(term_refs):
        feats = term_ref.shape[1]
        at = pl.ds(pl.multiple_of((half_ref[0] ^ e) * feats, feats), feats)
        term = lax.dot_general(
            d_ref[0, mine, :], w_ref[0, at, :], numbers, preferred_element_type=jnp.float32
        ) + lax.dot_general(
            d_ref[1, mine, :], w_ref[1, at, :], numbers, preferred_element_type=jnp.float32
        )
        term_ref[mine, :] = term.astype(jnp.bfloat16)


def input_grad(pieces, spots, w_gu, half, ratio, total, first, count, earlier, filled=()):
    _, owned, group = w_gu.shape
    feats = owned // ratio
    operands = [half, *[in_vmem(x) for x in pieces], in_vmem(w_gu), *earlier, *[in_vmem(x) for x in filled]]
    return pl.pallas_call(
        functools.partial(input_grad_kernel, spots, ratio + 1, first, count),
        in_specs=[pl.BlockSpec(memory_space=pltpu.SMEM)]
        + [pl.BlockSpec(memory_space=pltpu.VMEM)] * (len(pieces) + 1)
        + [pl.BlockSpec(memory_space=pl.ANY)] * len(earlier)
        + [pl.BlockSpec(memory_space=pltpu.VMEM)] * len(filled),
        out_specs=[pl.BlockSpec(memory_space=pltpu.VMEM)] * (ratio + 1),
        out_shape=[pltpu.VMEM((2, total, group), jnp.bfloat16)]
        + [pltpu.VMEM((total, feats), jnp.bfloat16)] * ratio,
        input_output_aliases={len(operands) - len(filled) + i: i for i in range(len(filled))},
        compiler_params=pltpu.CompilerParams(vmem_limit_bytes=16 * 1024 * 1024),
    )(*operands)


def weight_grad_kernel(scale, features_ref, d_ref, mask_ref, *refs):
    out_ref, marks_ref = refs[-2:]
    mark(marks_ref, mask_ref)
    out_ref[0] = scale * lax.dot_general(
        features_ref[...], d_ref[0], (((0,), (0,)), ((), ())), preferred_element_type=jnp.float32
    )


def weight_grad(which, features, d_both, scale, mask, marks_shape, earlier, grads=None):
    total, owned = features.shape
    group = d_both.shape[2]
    step = min(owned, 256)
    operands = [features, in_vmem(d_both), mask, earlier] + ([] if grads is None else [grads])
    return pl.pallas_call(
        functools.partial(weight_grad_kernel, scale),
        grid=(owned // step,),
        in_specs=[
            pl.BlockSpec((total, step), lambda i: (0, i)),
            pl.BlockSpec((1, total, group), lambda i: (which, 0, 0)),
            pl.BlockSpec(memory_space=pltpu.SMEM),
        ]
        + [pl.BlockSpec(memory_space=pl.ANY)] * (len(operands) - 3),
        out_specs=[
            pl.BlockSpec((1, step, group), lambda i: (which, i, 0)),
            pl.BlockSpec(marks_shape, lambda i: (0, 0)),
        ],
        out_shape=[
            jax.ShapeDtypeStruct((2, owned, group), jnp.float32),
            pltpu.VMEM(marks_shape, jnp.float32),
        ],
        input_output_aliases={} if grads is None else {4: 0},
        compiler_params=pltpu.CompilerParams(vmem_limit_bytes=16 * 1024 * 1024),
    )(*operands)


def body(tokens, gate_up_codes, gate_up_scales, d_hidden):
    rows, feats = tokens.shape
    nodes, places = lax.axis_size("node"), lax.axis_size("local")
    ratio = nodes // places
    _, owned, group = gate_up_codes.shape
    bits = [1 << b for b in range(places.bit_length() - 1)]
    node, place = lax.axis_index("node"), lax.axis_index("local")
    tokens, half, mask = lax.optimization_barrier(
        (tokens, (node & (ratio - 1))[None], ((node >> (ratio.bit_length() - 1)) ^ place)[None])
    )
    chunk = rows // CHUNKS
    part = chunk // 2
    orders = (bits, bits[::-1])

    def permute(x, move):
        return lax.ppermute(x, AXES, pairs(move, places, ratio))

    def own_features(x, marks):
        got = {j: permute(x, lambda p, h, q: (q ^ j, h, p)) for j in [*range(1, places), 0]}
        return jnp.stack([pick(got, k, marks) for k in range(places)])

    def joined(halves):
        def by_half(out_ref, i, value):
            for c in range(CHUNKS):
                out_ref[c, :, :, i * feats : (i + 1) * feats] = value[:, c * chunk : (c + 1) * chunk]

        return shuffle(dict(enumerate(halves)), half, (), (CHUNKS, places, chunk, owned), by_half)

    def sent(x, order, step):
        ks = [k for k in range(places) if not any(k & bit for bit in order[:step])]
        bit = order[step]
        away = [i for i, k in enumerate(ks) if k & bit]
        stay = [i for i, k in enumerate(ks) if not k & bit]
        out = jnp.stack([x[:, i] for i in away], axis=1).astype(jnp.bfloat16)
        keep = jnp.stack([x[:, i] for i in stay], axis=1).astype(jnp.float32)
        return keep, permute(out, lambda p, h, q: (p, h, q ^ bit))

    def start_forward(c):
        aways = [order[0] for order in orders]
        out, keep = other_halves(others, w_gu, own, half, c * chunk, chunk, aways)
        return keep, [
            permute(x, lambda p, h, q, bit=bit: (p, h, q ^ bit)) for x, bit in zip(out, aways)
        ]

    def next_sums(keep, got, step):
        summed = [k + g.astype(jnp.float32) for k, g in zip(keep, got)]
        return list(zip(*[sent(x, orders[s], step) for s, x in enumerate(summed)]))

    def gradients(keep, got, first):
        hidden, streams = [], []
        for k, g in zip(keep, got):
            gate, up = (k + g.astype(jnp.float32))[:, 0]
            sigmoid_gate = jax.nn.sigmoid(gate)
            active = gate * sigmoid_gate
            hidden.append((active * up).astype(jnp.bfloat16))
            grad_in = d_hidden[first : first + gate.shape[0]].astype(jnp.float32)
            first += gate.shape[0]
            d_gate = grad_in * up * sigmoid_gate * (1.0 + gate * (1.0 - sigmoid_gate))
            d_up = grad_in * active
            streams.append(jnp.stack([d_gate, d_up]).astype(jnp.bfloat16))
        return hidden, jnp.stack(streams)

    def send_direct(x):
        return {bit: permute(x, lambda p, h, q: (p, h, q ^ bit)) for bit in bits}

    def forward_rest(c, x, direct):
        pieces, spots = [x] + [direct[bit] for bit in bits], [(c * places + k) * chunk for k in [0] + bits]
        for s, order in enumerate(orders):
            held = {0: None}
            for bit in order:
                for k in list(held):
                    if k == 0:
                        held[bit] = direct[bit][s : s + 1]
                    else:
                        held[k ^ bit] = permute(held[k], lambda p, h, q: (p, h, q ^ bit))
                        pieces.append(held[k ^ bit])
                        spots.append((c * places + (k ^ bit)) * chunk + s * part)
        return pieces, spots

    w_gu, marks = dequant(gate_up_codes, gate_up_scales, mask, (places, feats))
    mine = own_features(tokens, marks)
    others = [permute(mine, lambda p, h, q, e=e: (p, h ^ e, q)) for e in range(1, ratio)]
    own = own_half(mine, w_gu, half)
    (keep_a, got_a), (keep_b, got_b) = start_forward(0), start_forward(1)
    for step in range(1, len(bits)):
        keep_a, got_a = next_sums(keep_a, got_a, step)
        keep_b, got_b = next_sums(keep_b, got_b, step)
    hidden_b, streams_b = gradients(keep_b, got_b, chunk)
    hidden_a, streams_a = gradients(keep_a, after(got_a, streams_b), 0)
    direct_a, direct_b = send_direct(streams_a), send_direct(streams_b)
    pieces_a, spots_a = forward_rest(0, streams_a, direct_a)
    pieces_b, spots_b = forward_rest(1, streams_b, direct_b)
    near, total, count = 1 + len(bits), places * rows, places * chunk
    filled = input_grad(
        pieces_b + pieces_a[:near],
        spots_b + spots_a[:near],
        w_gu, half, ratio, total, count, count, hidden_a + hidden_b,
    )
    d_all, *term = input_grad(
        pieces_a[near:], spots_a[near:], w_gu, half, ratio, total, 0, count, [], filled
    )
    summed = term[0].astype(jnp.float32)
    for e in range(1, ratio):
        got = permute(term[e], lambda p, h, q: (p, h ^ e, q))
        summed = summed + got.astype(jnp.float32)
    summed = summed.reshape(CHUNKS, places, chunk, feats).astype(jnp.bfloat16)
    summed = [summed[:, k].reshape(rows, feats) for k in range(places)]
    far_first = [*range(places // 2, places), *range(1, places // 2)]
    arrived = {k: permute(summed[k], lambda p, h, q: (p, h, q ^ k)) for k in range(1, places)}
    arrived[0] = summed[0]
    flat = joined([mine] + others).reshape(total, owned)
    scale = 1.0 / math.sqrt(rows * places)
    grads, marks = weight_grad(0, flat, d_all, scale, mask, marks.shape, summed[0][:16])
    arrived = [pick(arrived, j, marks) for j in range(places)]
    summands = [arrived[0]] + [
        permute(arrived[j], lambda p, h, q: (p ^ j, h, q)) for j in reversed(far_first)
    ]
    grads, marks = weight_grad(1, flat, d_all, scale, mask, marks.shape, arrived[0][:16], grads)
    summands[0] = after(summands[0], marks)
    d_tokens = sum(x.astype(jnp.float32) for x in summands).astype(jnp.bfloat16)
    return jnp.concatenate(hidden_a + hidden_b), d_tokens, grads


def solution(mesh):
    placed = (
        P("local", "node"),
        P(None, "local", "node"),
        P(None, "local", "node"),
        P("local", "node"),
    )
    return jax.shard_map(
        body,
        mesh=mesh,
        in_specs=placed,
        out_specs=(P("local", "node"), P("local", "node"), P(None, "local", "node")),
        check_vma=False,
    )
```

```python
import functools
import math

import jax
import jax.numpy as jnp
from jax import lax
from jax.experimental import pallas as pl
from jax.experimental.pallas import tpu as pltpu
from jax.sharding import PartitionSpec as P

BLOCK = 128
CHUNKS = 2
AXES = ("node", "local")


def in_vmem(x):
    return pltpu.with_memory_space_constraint(x, pltpu.VMEM)


def mark(marks_ref, mask_ref):
    for i in range(marks_ref.shape[0]):
        marks_ref[i : i + 1, :] = jnp.where(mask_ref[0] == i, 1.0, 0.0) * jnp.ones_like(marks_ref[:1, :])


def pick(choices, i, marks):
    out = choices[i]
    for m in reversed(range(1, len(choices))):
        out = jnp.where(marks[m : m + 1] > 0.5, choices[i ^ m], out)
    return out


def dequant_kernel(mask_ref, codes_ref, scales_ref, w_ref, marks_ref, narrow_ref, wide_ref, sem, scales_sem):
    mark(marks_ref, mask_ref)
    _, owned, group = w_ref.shape
    tile = 16

    def copy(b):
        at = pl.ds(b * BLOCK, BLOCK)
        return pltpu.make_async_copy(codes_ref.at[:, at, :], w_ref.at[:, at, :], sem.at[b])

    scales = pltpu.make_async_copy(scales_ref, narrow_ref, scales_sem)
    scales.start()
    for b in range(owned // BLOCK):
        copy(b).start()
    scales.wait()
    wide_ref[...] = narrow_ref[...].astype(jnp.float32)
    for b in range(owned // BLOCK):
        copy(b).wait()
        for g in range(2):
            scale = jnp.broadcast_to(wide_ref[g, b : b + 1, :], (tile, group)).astype(jnp.bfloat16)
            for t in range(b * BLOCK, (b + 1) * BLOCK, tile):
                w_ref[g, t : t + tile] = w_ref[g, t : t + tile] * scale


def dequant(codes, scales, mask, marks_shape):
    codes, scales = (pltpu.with_memory_space_constraint(x, pltpu.HBM) for x in (codes, scales))
    return pl.pallas_call(
        dequant_kernel,
        in_specs=[pl.BlockSpec(memory_space=pltpu.SMEM)] + [pl.BlockSpec(memory_space=pl.ANY)] * 2,
        out_specs=[pl.BlockSpec(memory_space=pltpu.VMEM)] * 2,
        out_shape=[
            pltpu.VMEM(codes.shape, jnp.bfloat16),
            pltpu.VMEM(marks_shape, jnp.float32),
        ],
        scratch_shapes=[
            pltpu.VMEM(scales.shape, jnp.bfloat16),
            pltpu.VMEM(scales.shape, jnp.float32),
            pltpu.SemaphoreType.DMA((codes.shape[1] // BLOCK,)),
            pltpu.SemaphoreType.DMA,
        ],
        compiler_params=pltpu.CompilerParams(vmem_limit_bytes=12 * 1024 * 1024),
    )(mask, codes, scales)


def pairs(move, places, ratio):
    out = []
    for plane in range(places):
        for half in range(ratio):
            for place in range(places):
                p, h, q = move(plane, half, place)
                out.append(
                    ((plane * ratio + half) * places + place, (p * ratio + h) * places + q)
                )
    return out


def after(x, earlier):
    return lax.optimization_barrier((x, earlier))[0]


def shuffle_kernel(order, write, index_ref, *refs):
    count = len(order)
    choices, outs = refs[:count], refs[-1:] if write else refs[-count:]
    for i in range(count):
        for j, choice in zip(order, choices):

            @pl.when(index_ref[0] == i ^ j)
            def _():
                if write:
                    write(outs[0], i, choice[...])
                else:
                    outs[i][...] = choice[...]


def shuffle(choices, index, earlier=(), shape=None, write=None):
    one = choices[0]
    shapes = [shape] if write else [one.shape] * len(choices)
    out = pl.pallas_call(
        functools.partial(shuffle_kernel, list(choices), write),
        in_specs=[pl.BlockSpec(memory_space=pltpu.SMEM)]
        + [pl.BlockSpec(memory_space=pltpu.VMEM)] * len(choices)
        + [pl.BlockSpec(memory_space=pl.ANY)] * len(earlier),
        out_specs=[pl.BlockSpec(memory_space=pltpu.VMEM)] * len(shapes),
        out_shape=[pltpu.VMEM(s, one.dtype) for s in shapes],
        compiler_params=pltpu.CompilerParams(vmem_limit_bytes=16 * 1024 * 1024),
    )(index, *[in_vmem(x) for x in choices.values()], *earlier)
    return out[0] if write else list(out)


def own_half_kernel(first, half_ref, x_ref, w_ref, out_ref):
    _, places, chunk, _ = out_ref.shape
    feats = x_ref.shape[2]
    at = pl.ds(pl.multiple_of(half_ref[0] * feats, feats), feats)
    flat = x_ref[:, pl.ds(first, chunk), :].reshape(places * chunk, feats)
    for g in range(2):
        out_ref[g] = jnp.dot(flat, w_ref[g, at, :], preferred_element_type=jnp.float32).reshape(
            out_ref.shape[1:]
        )


def own_half(x, w_gu, half, first, chunk):
    places = x.shape[0]
    return pl.pallas_call(
        functools.partial(own_half_kernel, first),
        in_specs=[pl.BlockSpec(memory_space=pltpu.SMEM)] + [pl.BlockSpec(memory_space=pltpu.VMEM)] * 2,
        out_specs=pl.BlockSpec(memory_space=pltpu.VMEM),
        out_shape=pltpu.VMEM((2, places, chunk, w_gu.shape[2]), jnp.float32),
        compiler_params=pltpu.CompilerParams(vmem_limit_bytes=12 * 1024 * 1024),
    )(half, in_vmem(x), in_vmem(w_gu))


def partial_sums_kernel(es, summed, first, chunk, aways, half_ref, *refs):
    xs, w_ref, outs = refs[: len(es)], refs[len(es)], refs[-2 * len(aways) :]
    places, _, feats = xs[0].shape
    part = chunk // len(aways)
    rows = pl.ds(first, chunk)
    for g in range(2):
        total = refs[len(es) + 1][g].reshape(places * chunk, -1) if summed else 0.0
        for e, x_ref in zip(es, xs):
            at = pl.ds(pl.multiple_of((half_ref[0] ^ e) * feats, feats), feats)
            flat = x_ref[:, rows, :].reshape(places * chunk, feats)
            total += jnp.dot(flat, w_ref[g, at, :], preferred_element_type=jnp.float32)
        for s, away in enumerate(aways):
            counts = [0, 0]
            for k in range(places):
                block = total[k * chunk + s * part : k * chunk + (s + 1) * part]
                kind = 0 if k & away else 1
                out_ref = outs[2 * s + kind]
                out_ref[g, counts[kind]] = block.astype(out_ref.dtype)
                counts[kind] += 1


def partial_sums(xs, w_gu, summed, half, first, chunk, aways):
    places, group = xs[max(xs)].shape[0], w_gu.shape[2]
    shape = (2, places // 2, chunk // len(aways), group)
    operands = [*xs.values(), w_gu, *summed]
    outs = pl.pallas_call(
        functools.partial(partial_sums_kernel, list(xs), bool(summed), first, chunk, aways),
        in_specs=[pl.BlockSpec(memory_space=pltpu.SMEM)]
        + [pl.BlockSpec(memory_space=pltpu.VMEM)] * len(operands),
        out_specs=[pl.BlockSpec(memory_space=pltpu.VMEM)] * (2 * len(aways)),
        out_shape=[pltpu.VMEM(shape, jnp.bfloat16), pltpu.VMEM(shape, jnp.float32)] * len(aways),
        compiler_params=pltpu.CompilerParams(vmem_limit_bytes=16 * 1024 * 1024),
    )(half, *[in_vmem(x) for x in operands])
    return outs[0::2], outs[1::2]


def input_grad_kernel(spots, es, first, count, half_ref, *refs):
    pieces, w_ref = refs[: len(spots)], refs[len(spots)]
    d_ref, *term_refs = refs[len(refs) - 1 - len(es) :]
    for piece, row in zip(pieces, spots):
        streams, _, part, _ = piece.shape
        for s in range(streams):
            d_ref[:, pl.ds(row + s * part, part), :] = piece[s]
    mine = pl.ds(first, count)
    numbers = (((1,), (1,)), ((), ()))
    for e, term_ref in zip(es, term_refs):
        feats = term_ref.shape[1]
        at = pl.ds(pl.multiple_of((half_ref[0] ^ e) * feats, feats), feats)
        term = lax.dot_general(
            d_ref[0, mine, :], w_ref[0, at, :], numbers, preferred_element_type=jnp.float32
        ) + lax.dot_general(
            d_ref[1, mine, :], w_ref[1, at, :], numbers, preferred_element_type=jnp.float32
        )
        term_ref[mine, :] = term.astype(jnp.bfloat16)


def input_grad(pieces, spots, w_gu, half, es, ratio, total, first, count, earlier, filled=()):
    _, owned, group = w_gu.shape
    feats = owned // ratio
    operands = [half, *[in_vmem(x) for x in pieces], in_vmem(w_gu), *earlier, *[in_vmem(x) for x in filled]]
    return pl.pallas_call(
        functools.partial(input_grad_kernel, spots, es, first, count),
        in_specs=[pl.BlockSpec(memory_space=pltpu.SMEM)]
        + [pl.BlockSpec(memory_space=pltpu.VMEM)] * (len(pieces) + 1)
        + [pl.BlockSpec(memory_space=pl.ANY)] * len(earlier)
        + [pl.BlockSpec(memory_space=pltpu.VMEM)] * len(filled),
        out_specs=[pl.BlockSpec(memory_space=pltpu.VMEM)] * (len(es) + 1),
        out_shape=[pltpu.VMEM((2, total, group), jnp.bfloat16)]
        + [pltpu.VMEM((total, feats), jnp.bfloat16)] * len(es),
        input_output_aliases={len(operands) - len(filled) + i: i for i in range(len(filled))},
        compiler_params=pltpu.CompilerParams(vmem_limit_bytes=16 * 1024 * 1024),
    )(*operands)


def weight_grad_kernel(scale, features_ref, d_ref, mask_ref, *refs):
    out_ref, marks_ref = refs[-2:]
    mark(marks_ref, mask_ref)
    out_ref[0] = scale * lax.dot_general(
        features_ref[...], d_ref[0], (((0,), (0,)), ((), ())), preferred_element_type=jnp.float32
    )


def weight_grad(which, features, d_both, scale, mask, marks_shape, earlier, grads=None):
    total, owned = features.shape
    group = d_both.shape[2]
    step = min(owned, 256)
    operands = [features, in_vmem(d_both), mask, earlier] + ([] if grads is None else [grads])
    return pl.pallas_call(
        functools.partial(weight_grad_kernel, scale),
        grid=(owned // step,),
        in_specs=[
            pl.BlockSpec((total, step), lambda i: (0, i)),
            pl.BlockSpec((1, total, group), lambda i: (which, 0, 0)),
            pl.BlockSpec(memory_space=pltpu.SMEM),
        ]
        + [pl.BlockSpec(memory_space=pl.ANY)] * (len(operands) - 3),
        out_specs=[
            pl.BlockSpec((1, step, group), lambda i: (which, i, 0)),
            pl.BlockSpec(marks_shape, lambda i: (0, 0)),
        ],
        out_shape=[
            jax.ShapeDtypeStruct((2, owned, group), jnp.float32),
            pltpu.VMEM(marks_shape, jnp.float32),
        ],
        input_output_aliases={} if grads is None else {4: 0},
        compiler_params=pltpu.CompilerParams(vmem_limit_bytes=16 * 1024 * 1024),
    )(*operands)


def body(tokens, gate_up_codes, gate_up_scales, d_hidden):
    rows, feats = tokens.shape
    nodes, places = lax.axis_size("node"), lax.axis_size("local")
    ratio = nodes // places
    _, owned, group = gate_up_codes.shape
    bits = [1 << b for b in range(places.bit_length() - 1)]
    node, place = lax.axis_index("node"), lax.axis_index("local")
    tokens, half, mask = lax.optimization_barrier(
        (tokens, (node & (ratio - 1))[None], ((node >> (ratio.bit_length() - 1)) ^ place)[None])
    )
    chunk = rows // CHUNKS
    part = chunk // 2
    orders = (bits, bits[::-1])

    def permute(x, move):
        return lax.ppermute(x, AXES, pairs(move, places, ratio))

    def own_features(x, marks):
        got = {j: permute(x, lambda p, h, q: (q ^ j, h, p)) for j in [*range(1, places), 0]}
        return jnp.stack([pick(got, k, marks) for k in range(places)])

    def joined(halves):
        def by_half(out_ref, i, value):
            for c in range(CHUNKS):
                out_ref[c, :, :, i * feats : (i + 1) * feats] = value[:, c * chunk : (c + 1) * chunk]

        return shuffle(dict(enumerate(halves)), half, (), (CHUNKS, places, chunk, owned), by_half)

    def sent(x, order, step):
        ks = [k for k in range(places) if not any(k & bit for bit in order[:step])]
        bit = order[step]
        away = [i for i, k in enumerate(ks) if k & bit]
        stay = [i for i, k in enumerate(ks) if not k & bit]
        out = jnp.stack([x[:, i] for i in away], axis=1).astype(jnp.bfloat16)
        keep = jnp.stack([x[:, i] for i in stay], axis=1).astype(jnp.float32)
        return keep, permute(out, lambda p, h, q: (p, h, q ^ bit))

    def start_forward(c, early):
        aways = [order[0] for order in orders]
        xs = dict(enumerate([mine] + others))
        summed = [own_half(xs.pop(0), w_gu, half, c * chunk, chunk)] if early else []
        out, keep = partial_sums(xs, w_gu, summed, half, c * chunk, chunk, aways)
        return keep, [
            permute(x, lambda p, h, q, bit=bit: (p, h, q ^ bit)) for x, bit in zip(out, aways)
        ]

    def next_sums(keep, got, step):
        summed = [k + g.astype(jnp.float32) for k, g in zip(keep, got)]
        return list(zip(*[sent(x, orders[s], step) for s, x in enumerate(summed)]))

    def gradients(keep, got, first):
        hidden, streams = [], []
        for k, g in zip(keep, got):
            gate, up = (k + g.astype(jnp.float32))[:, 0]
            sigmoid_gate = jax.nn.sigmoid(gate)
            active = gate * sigmoid_gate
            hidden.append((active * up).astype(jnp.bfloat16))
            grad_in = d_hidden[first : first + gate.shape[0]].astype(jnp.float32)
            first += gate.shape[0]
            d_gate = grad_in * up * sigmoid_gate * (1.0 + gate * (1.0 - sigmoid_gate))
            d_up = grad_in * active
            streams.append(jnp.stack([d_gate, d_up]).astype(jnp.bfloat16))
        return hidden, jnp.stack(streams)

    def send_direct(x):
        return {bit: permute(x, lambda p, h, q: (p, h, q ^ bit)) for bit in bits}

    def forward_rest(c, x, direct):
        pieces, spots = [x] + [direct[bit] for bit in bits], [(c * places + k) * chunk for k in [0] + bits]
        for s, order in enumerate(orders):
            held = {0: None}
            for bit in order:
                for k in list(held):
                    if k == 0:
                        held[bit] = direct[bit][s : s + 1]
                    else:
                        held[k ^ bit] = permute(held[k], lambda p, h, q: (p, h, q ^ bit))
                        pieces.append(held[k ^ bit])
                        spots.append((c * places + (k ^ bit)) * chunk + s * part)
        return pieces, spots

    w_gu, marks = dequant(gate_up_codes, gate_up_scales, mask, (places, feats))
    mine = own_features(tokens, marks)
    others = [permute(mine, lambda p, h, q, e=e: (p, h ^ e, q)) for e in range(1, ratio)]
    (keep_a, got_a), (keep_b, got_b) = start_forward(0, False), start_forward(1, True)
    for step in range(1, len(bits)):
        keep_a, got_a = next_sums(keep_a, got_a, step)
        keep_b, got_b = next_sums(keep_b, got_b, step)
    hidden_b, streams_b = gradients(keep_b, got_b, chunk)
    hidden_a, streams_a = gradients(keep_a, after(got_a, streams_b), 0)
    direct_a, direct_b = send_direct(streams_a), send_direct(streams_b)
    pieces_a, spots_a = forward_rest(0, streams_a, direct_a)
    pieces_b, spots_b = forward_rest(1, streams_b, direct_b)
    near, total, count = 1 + len(bits), places * rows, places * chunk
    d_all, own_term, *other_terms = input_grad(
        pieces_b + pieces_a[:near],
        spots_b + spots_a[:near],
        w_gu, half, list(range(ratio)), ratio, total, count, count, hidden_a + hidden_b,
    )
    d_all, *other_terms = input_grad(
        pieces_a[near:],
        spots_a[near:],
        w_gu, half, list(range(1, ratio)), ratio, total, 0, count, [], [d_all, *other_terms],
    )
    d_all, own_term = input_grad([], [], w_gu, half, [0], ratio, total, 0, count, [], [d_all, own_term])
    summed = own_term.astype(jnp.float32)
    for e, term in enumerate(other_terms, 1):
        got = permute(term, lambda p, h, q: (p, h ^ e, q))
        summed = summed + got.astype(jnp.float32)
    summed = summed.reshape(CHUNKS, places, chunk, feats).astype(jnp.bfloat16)
    summed = [summed[:, k].reshape(rows, feats) for k in range(places)]
    far_first = [*range(places // 2, places), *range(1, places // 2)]
    arrived = {k: permute(summed[k], lambda p, h, q: (p, h, q ^ k)) for k in range(1, places)}
    arrived[0] = summed[0]
    flat = joined([mine] + others).reshape(total, owned)
    scale = 1.0 / math.sqrt(rows * places)
    grads, marks = weight_grad(0, flat, d_all, scale, mask, marks.shape, summed[0][:16])
    arrived = [pick(arrived, j, marks) for j in range(places)]
    summands = [arrived[0]] + [
        permute(arrived[j], lambda p, h, q: (p ^ j, h, q)) for j in reversed(far_first)
    ]
    grads, marks = weight_grad(1, flat, d_all, scale, mask, marks.shape, arrived[0][:16], grads)
    summands[0] = after(summands[0], marks)
    d_tokens = sum(x.astype(jnp.float32) for x in summands).astype(jnp.bfloat16)
    return jnp.concatenate(hidden_a + hidden_b), d_tokens, grads


def solution(mesh):
    placed = (
        P("local", "node"),
        P(None, "local", "node"),
        P(None, "local", "node"),
        P("local", "node"),
    )
    return jax.shard_map(
        body,
        mesh=mesh,
        in_specs=placed,
        out_specs=(P("local", "node"), P("local", "node"), P(None, "local", "node")),
        check_vma=False,
    )
```

```python
import functools
import math

import jax
import jax.numpy as jnp
from jax import lax
from jax.experimental import pallas as pl
from jax.experimental.pallas import tpu as pltpu
from jax.sharding import PartitionSpec as P

BLOCK = 128
CHUNKS = 2
AXES = ("node", "local")


def in_vmem(x):
    return pltpu.with_memory_space_constraint(x, pltpu.VMEM)


def mark(marks_ref, mask_ref):
    for i in range(marks_ref.shape[0]):
        marks_ref[i : i + 1, :] = jnp.where(mask_ref[0] == i, 1.0, 0.0) * jnp.ones_like(marks_ref[:1, :])


def pick(choices, i, marks):
    out = choices[i]
    for m in reversed(range(1, len(choices))):
        out = jnp.where(marks[m : m + 1] > 0.5, choices[i ^ m], out)
    return out


def dequant_kernel(mask_ref, codes_ref, scales_ref, w_ref, marks_ref, wide_ref, sem):
    mark(marks_ref, mask_ref)
    _, owned, group = w_ref.shape
    tile = 16

    def copy(b):
        at = pl.ds(b * BLOCK, BLOCK)
        return pltpu.make_async_copy(codes_ref.at[:, at, :], w_ref.at[:, at, :], sem.at[b])

    for b in range(owned // BLOCK):
        copy(b).start()
    wide_ref[...] = scales_ref[...].astype(jnp.float32)
    for b in range(owned // BLOCK):
        copy(b).wait()
        for g in range(2):
            scale = jnp.broadcast_to(wide_ref[g, b : b + 1, :], (tile, group)).astype(jnp.bfloat16)
            for t in range(b * BLOCK, (b + 1) * BLOCK, tile):
                w_ref[g, t : t + tile] = w_ref[g, t : t + tile] * scale


def dequant(codes, scales, mask, marks_shape):
    codes = pltpu.with_memory_space_constraint(codes, pltpu.HBM)
    return pl.pallas_call(
        dequant_kernel,
        in_specs=[
            pl.BlockSpec(memory_space=pltpu.SMEM),
            pl.BlockSpec(memory_space=pl.ANY),
            pl.BlockSpec(memory_space=pltpu.VMEM),
        ],
        out_specs=[pl.BlockSpec(memory_space=pltpu.VMEM)] * 2,
        out_shape=[
            pltpu.VMEM(codes.shape, jnp.bfloat16),
            pltpu.VMEM(marks_shape, jnp.float32),
        ],
        scratch_shapes=[
            pltpu.VMEM(scales.shape, jnp.float32),
            pltpu.SemaphoreType.DMA((codes.shape[1] // BLOCK,)),
        ],
        compiler_params=pltpu.CompilerParams(vmem_limit_bytes=12 * 1024 * 1024),
    )(mask, codes, in_vmem(scales))


def pairs(move, places, ratio):
    out = []
    for plane in range(places):
        for half in range(ratio):
            for place in range(places):
                p, h, q = move(plane, half, place)
                out.append(
                    ((plane * ratio + half) * places + place, (p * ratio + h) * places + q)
                )
    return out


def after(x, earlier):
    return lax.optimization_barrier((x, earlier))[0]


def shuffle_kernel(order, write, index_ref, *refs):
    count = len(order)
    choices, outs = refs[:count], refs[-1:] if write else refs[-count:]
    for i in range(count):
        for j, choice in zip(order, choices):

            @pl.when(index_ref[0] == i ^ j)
            def _():
                if write:
                    write(outs[0], i, choice[...])
                else:
                    outs[i][...] = choice[...]


def shuffle(choices, index, earlier=(), shape=None, write=None):
    one = choices[0]
    shapes = [shape] if write else [one.shape] * len(choices)
    out = pl.pallas_call(
        functools.partial(shuffle_kernel, list(choices), write),
        in_specs=[pl.BlockSpec(memory_space=pltpu.SMEM)]
        + [pl.BlockSpec(memory_space=pltpu.VMEM)] * len(choices)
        + [pl.BlockSpec(memory_space=pl.ANY)] * len(earlier),
        out_specs=[pl.BlockSpec(memory_space=pltpu.VMEM)] * len(shapes),
        out_shape=[pltpu.VMEM(s, one.dtype) for s in shapes],
        compiler_params=pltpu.CompilerParams(vmem_limit_bytes=16 * 1024 * 1024),
    )(index, *[in_vmem(x) for x in choices.values()], *earlier)
    return out[0] if write else list(out)


def own_half_kernel(first, half_ref, x_ref, w_ref, out_ref):
    _, places, chunk, _ = out_ref.shape
    feats = x_ref.shape[2]
    at = pl.ds(pl.multiple_of(half_ref[0] * feats, feats), feats)
    flat = x_ref[:, pl.ds(first, chunk), :].reshape(places * chunk, feats)
    for g in range(2):
        out_ref[g] = jnp.dot(flat, w_ref[g, at, :], preferred_element_type=jnp.float32).reshape(
            out_ref.shape[1:]
        )


def own_half(x, w_gu, half, first, chunk):
    places = x.shape[0]
    return pl.pallas_call(
        functools.partial(own_half_kernel, first),
        in_specs=[pl.BlockSpec(memory_space=pltpu.SMEM)] + [pl.BlockSpec(memory_space=pltpu.VMEM)] * 2,
        out_specs=pl.BlockSpec(memory_space=pltpu.VMEM),
        out_shape=pltpu.VMEM((2, places, chunk, w_gu.shape[2]), jnp.float32),
        compiler_params=pltpu.CompilerParams(vmem_limit_bytes=12 * 1024 * 1024),
    )(half, in_vmem(x), in_vmem(w_gu))


def partial_sums_kernel(es, summed, first, chunk, aways, half_ref, *refs):
    xs, w_ref, outs = refs[: len(es)], refs[len(es)], refs[-2 * len(aways) :]
    places, _, feats = xs[0].shape
    part = chunk // len(aways)
    rows = pl.ds(first, chunk)
    for g in range(2):
        total = refs[len(es) + 1][g].reshape(places * chunk, -1) if summed else 0.0
        for e, x_ref in zip(es, xs):
            at = pl.ds(pl.multiple_of((half_ref[0] ^ e) * feats, feats), feats)
            flat = x_ref[:, rows, :].reshape(places * chunk, feats)
            total += jnp.dot(flat, w_ref[g, at, :], preferred_element_type=jnp.float32)
        for s, away in enumerate(aways):
            counts = [0, 0]
            for k in range(places):
                block = total[k * chunk + s * part : k * chunk + (s + 1) * part]
                kind = 0 if k & away else 1
                out_ref = outs[2 * s + kind]
                out_ref[g, counts[kind]] = block.astype(out_ref.dtype)
                counts[kind] += 1


def partial_sums(xs, w_gu, summed, half, first, chunk, aways):
    places, group = xs[max(xs)].shape[0], w_gu.shape[2]
    shape = (2, places // 2, chunk // len(aways), group)
    operands = [*xs.values(), w_gu, *summed]
    outs = pl.pallas_call(
        functools.partial(partial_sums_kernel, list(xs), bool(summed), first, chunk, aways),
        in_specs=[pl.BlockSpec(memory_space=pltpu.SMEM)]
        + [pl.BlockSpec(memory_space=pltpu.VMEM)] * len(operands),
        out_specs=[pl.BlockSpec(memory_space=pltpu.VMEM)] * (2 * len(aways)),
        out_shape=[pltpu.VMEM(shape, jnp.bfloat16), pltpu.VMEM(shape, jnp.float32)] * len(aways),
        compiler_params=pltpu.CompilerParams(vmem_limit_bytes=16 * 1024 * 1024),
    )(half, *[in_vmem(x) for x in operands])
    return outs[0::2], outs[1::2]


def input_grad_kernel(spots, es, first, count, half_ref, *refs):
    pieces, w_ref = refs[: len(spots)], refs[len(spots)]
    d_ref, *term_refs = refs[len(refs) - 1 - len(es) :]
    for piece, row in zip(pieces, spots):
        streams, _, part, _ = piece.shape
        for s in range(streams):
            d_ref[:, pl.ds(row + s * part, part), :] = piece[s]
    mine = pl.ds(first, count)
    numbers = (((1,), (1,)), ((), ()))
    for e, term_ref in zip(es, term_refs):
        feats = term_ref.shape[1]
        at = pl.ds(pl.multiple_of((half_ref[0] ^ e) * feats, feats), feats)
        term = lax.dot_general(
            d_ref[0, mine, :], w_ref[0, at, :], numbers, preferred_element_type=jnp.float32
        ) + lax.dot_general(
            d_ref[1, mine, :], w_ref[1, at, :], numbers, preferred_element_type=jnp.float32
        )
        term_ref[mine, :] = term.astype(jnp.bfloat16)


def input_grad(pieces, spots, w_gu, half, es, ratio, total, first, count, earlier, filled=()):
    _, owned, group = w_gu.shape
    feats = owned // ratio
    operands = [half, *[in_vmem(x) for x in pieces], in_vmem(w_gu), *earlier, *[in_vmem(x) for x in filled]]
    return pl.pallas_call(
        functools.partial(input_grad_kernel, spots, es, first, count),
        in_specs=[pl.BlockSpec(memory_space=pltpu.SMEM)]
        + [pl.BlockSpec(memory_space=pltpu.VMEM)] * (len(pieces) + 1)
        + [pl.BlockSpec(memory_space=pl.ANY)] * len(earlier)
        + [pl.BlockSpec(memory_space=pltpu.VMEM)] * len(filled),
        out_specs=[pl.BlockSpec(memory_space=pltpu.VMEM)] * (len(es) + 1),
        out_shape=[pltpu.VMEM((2, total, group), jnp.bfloat16)]
        + [pltpu.VMEM((total, feats), jnp.bfloat16)] * len(es),
        input_output_aliases={len(operands) - len(filled) + i: i for i in range(len(filled))},
        compiler_params=pltpu.CompilerParams(vmem_limit_bytes=16 * 1024 * 1024),
    )(*operands)


def weight_grad_kernel(scale, features_ref, d_ref, mask_ref, *refs):
    out_ref, marks_ref = refs[-2:]
    mark(marks_ref, mask_ref)
    out_ref[0] = scale * lax.dot_general(
        features_ref[...], d_ref[0], (((0,), (0,)), ((), ())), preferred_element_type=jnp.float32
    )


def weight_grad(which, features, d_both, scale, mask, marks_shape, earlier, grads=None):
    total, owned = features.shape
    group = d_both.shape[2]
    step = min(owned, 256)
    operands = [features, in_vmem(d_both), mask, earlier] + ([] if grads is None else [grads])
    return pl.pallas_call(
        functools.partial(weight_grad_kernel, scale),
        grid=(owned // step,),
        in_specs=[
            pl.BlockSpec((total, step), lambda i: (0, i)),
            pl.BlockSpec((1, total, group), lambda i: (which, 0, 0)),
            pl.BlockSpec(memory_space=pltpu.SMEM),
        ]
        + [pl.BlockSpec(memory_space=pl.ANY)] * (len(operands) - 3),
        out_specs=[
            pl.BlockSpec((1, step, group), lambda i: (which, i, 0)),
            pl.BlockSpec(marks_shape, lambda i: (0, 0)),
        ],
        out_shape=[
            jax.ShapeDtypeStruct((2, owned, group), jnp.float32),
            pltpu.VMEM(marks_shape, jnp.float32),
        ],
        input_output_aliases={} if grads is None else {4: 0},
        compiler_params=pltpu.CompilerParams(vmem_limit_bytes=16 * 1024 * 1024),
    )(*operands)


def body(tokens, gate_up_codes, gate_up_scales, d_hidden):
    rows, feats = tokens.shape
    nodes, places = lax.axis_size("node"), lax.axis_size("local")
    ratio = nodes // places
    _, owned, group = gate_up_codes.shape
    bits = [1 << b for b in range(places.bit_length() - 1)]
    node, place = lax.axis_index("node"), lax.axis_index("local")
    tokens, half, mask = lax.optimization_barrier(
        (tokens, (node & (ratio - 1))[None], ((node >> (ratio.bit_length() - 1)) ^ place)[None])
    )
    chunk = rows // CHUNKS
    part = chunk // 2
    orders = (bits, bits[::-1])

    def permute(x, move):
        return lax.ppermute(x, AXES, pairs(move, places, ratio))

    def own_features(x, marks):
        got = {j: permute(x, lambda p, h, q: (q ^ j, h, p)) for j in [*range(1, places), 0]}
        return jnp.stack([pick(got, k, marks) for k in range(places)])

    def joined(halves):
        def by_half(out_ref, i, value):
            for c in range(CHUNKS):
                out_ref[c, :, :, i * feats : (i + 1) * feats] = value[:, c * chunk : (c + 1) * chunk]

        return shuffle(dict(enumerate(halves)), half, (), (CHUNKS, places, chunk, owned), by_half)

    def sent(x, order, step):
        ks = [k for k in range(places) if not any(k & bit for bit in order[:step])]
        bit = order[step]
        away = [i for i, k in enumerate(ks) if k & bit]
        stay = [i for i, k in enumerate(ks) if not k & bit]
        out = jnp.stack([x[:, i] for i in away], axis=1).astype(jnp.bfloat16)
        keep = jnp.stack([x[:, i] for i in stay], axis=1).astype(jnp.float32)
        return keep, permute(out, lambda p, h, q: (p, h, q ^ bit))

    def start_forward(c, early):
        aways = [order[0] for order in orders]
        xs = dict(enumerate([mine] + others))
        summed = [own_half(xs.pop(0), w_gu, half, c * chunk, chunk)] if early else []
        out, keep = partial_sums(xs, w_gu, summed, half, c * chunk, chunk, aways)
        return keep, [
            permute(x, lambda p, h, q, bit=bit: (p, h, q ^ bit)) for x, bit in zip(out, aways)
        ]

    def next_sums(keep, got, step):
        summed = [k + g.astype(jnp.float32) for k, g in zip(keep, got)]
        return list(zip(*[sent(x, orders[s], step) for s, x in enumerate(summed)]))

    def gradients(keep, got, first):
        hidden, streams = [], []
        for k, g in zip(keep, got):
            gate, up = (k + g.astype(jnp.float32))[:, 0]
            sigmoid_gate = jax.nn.sigmoid(gate)
            active = gate * sigmoid_gate
            hidden.append((active * up).astype(jnp.bfloat16))
            grad_in = d_hidden[first : first + gate.shape[0]].astype(jnp.float32)
            first += gate.shape[0]
            d_gate = grad_in * up * sigmoid_gate * (1.0 + gate * (1.0 - sigmoid_gate))
            d_up = grad_in * active
            streams.append(jnp.stack([d_gate, d_up]).astype(jnp.bfloat16))
        return hidden, jnp.stack(streams)

    def send_direct(x):
        return {bit: permute(x, lambda p, h, q: (p, h, q ^ bit)) for bit in bits}

    def forward_rest(c, x, direct):
        pieces, spots = [x] + [direct[bit] for bit in bits], [(c * places + k) * chunk for k in [0] + bits]
        for s, order in enumerate(orders):
            held = {0: None}
            for bit in order:
                for k in list(held):
                    if k == 0:
                        held[bit] = direct[bit][s : s + 1]
                    else:
                        held[k ^ bit] = permute(held[k], lambda p, h, q: (p, h, q ^ bit))
                        pieces.append(held[k ^ bit])
                        spots.append((c * places + (k ^ bit)) * chunk + s * part)
        return pieces, spots

    w_gu, marks = dequant(gate_up_codes, gate_up_scales, mask, (places, feats))
    mine = own_features(tokens, marks)
    others = [permute(mine, lambda p, h, q, e=e: (p, h ^ e, q)) for e in range(1, ratio)]
    (keep_a, got_a), (keep_b, got_b) = start_forward(0, False), start_forward(1, True)
    for step in range(1, len(bits)):
        keep_a, got_a = next_sums(keep_a, got_a, step)
        keep_b, got_b = next_sums(keep_b, got_b, step)
    hidden_b, streams_b = gradients(keep_b, got_b, chunk)
    hidden_a, streams_a = gradients(keep_a, after(got_a, streams_b), 0)
    direct_a, direct_b = send_direct(streams_a), send_direct(streams_b)
    pieces_a, spots_a = forward_rest(0, streams_a, direct_a)
    pieces_b, spots_b = forward_rest(1, streams_b, direct_b)
    near, total, count = 1 + len(bits), places * rows, places * chunk
    d_all, own_term, *other_terms = input_grad(
        pieces_b + pieces_a[:near],
        spots_b + spots_a[:near],
        w_gu, half, list(range(ratio)), ratio, total, count, count, hidden_a + hidden_b,
    )
    d_all, *other_terms = input_grad(
        pieces_a[near:],
        spots_a[near:],
        w_gu, half, list(range(1, ratio)), ratio, total, 0, count, [], [d_all, *other_terms],
    )
    d_all, own_term = input_grad([], [], w_gu, half, [0], ratio, total, 0, count, [], [d_all, own_term])
    summed = own_term.astype(jnp.float32)
    for e, term in enumerate(other_terms, 1):
        got = permute(term, lambda p, h, q: (p, h ^ e, q))
        summed = summed + got.astype(jnp.float32)
    summed = summed.reshape(CHUNKS, places, chunk, feats).astype(jnp.bfloat16)
    summed = [summed[:, k].reshape(rows, feats) for k in range(places)]
    far_first = [*range(places // 2, places), *range(1, places // 2)]
    arrived = {k: permute(summed[k], lambda p, h, q: (p, h, q ^ k)) for k in range(1, places)}
    arrived[0] = summed[0]
    flat = joined([mine] + others).reshape(total, owned)
    scale = 1.0 / math.sqrt(rows * places)
    grads, marks = weight_grad(0, flat, d_all, scale, mask, marks.shape, summed[0][:16])
    arrived = [pick(arrived, j, marks) for j in range(places)]
    summands = [arrived[0]] + [
        permute(arrived[j], lambda p, h, q: (p ^ j, h, q)) for j in reversed(far_first)
    ]
    grads, marks = weight_grad(1, flat, d_all, scale, mask, marks.shape, arrived[0][:16], grads)
    summands[0] = after(summands[0], marks)
    d_tokens = sum(x.astype(jnp.float32) for x in summands).astype(jnp.bfloat16)
    return jnp.concatenate(hidden_a + hidden_b), d_tokens, grads


def solution(mesh):
    placed = (
        P("local", "node"),
        P(None, "local", "node"),
        P(None, "local", "node"),
        P("local", "node"),
    )
    return jax.shard_map(
        body,
        mesh=mesh,
        in_specs=placed,
        out_specs=(P("local", "node"), P("local", "node"), P(None, "local", "node")),
        check_vma=False,
    )
```

```python
import functools
import math

import jax
import jax.numpy as jnp
from jax import lax
from jax.experimental import pallas as pl
from jax.experimental.pallas import tpu as pltpu
from jax.sharding import PartitionSpec as P

BLOCK = 128
CHUNKS = 2
GRAD_ROWS = 256
AXES = ("node", "local")


def in_vmem(x):
    return pltpu.with_memory_space_constraint(x, pltpu.VMEM)


def mark(marks_ref, mask_ref):
    for i in range(marks_ref.shape[0]):
        marks_ref[i : i + 1, :] = jnp.where(mask_ref[0] == i, 1.0, 0.0) * jnp.ones_like(marks_ref[:1, :])


def pick(choices, i, marks):
    out = choices[i]
    for m in reversed(range(1, len(choices))):
        out = jnp.where(marks[m : m + 1] > 0.5, choices[i ^ m], out)
    return out


def dequant_kernel(mask_ref, codes_ref, scales_ref, w_ref, marks_ref, wide_ref, sem):
    mark(marks_ref, mask_ref)
    _, owned, group = w_ref.shape
    tile = 16

    def copy(b):
        at = pl.ds(b * BLOCK, BLOCK)
        return pltpu.make_async_copy(codes_ref.at[:, at, :], w_ref.at[:, at, :], sem.at[b])

    for b in range(owned // BLOCK):
        copy(b).start()
    wide_ref[...] = scales_ref[...].astype(jnp.float32)
    for b in range(owned // BLOCK):
        copy(b).wait()
        for g in range(2):
            scale = jnp.broadcast_to(wide_ref[g, b : b + 1, :], (tile, group)).astype(jnp.bfloat16)
            for t in range(b * BLOCK, (b + 1) * BLOCK, tile):
                w_ref[g, t : t + tile] = w_ref[g, t : t + tile] * scale


def dequant(codes, scales, mask, marks_shape):
    codes = pltpu.with_memory_space_constraint(codes, pltpu.HBM)
    return pl.pallas_call(
        dequant_kernel,
        in_specs=[
            pl.BlockSpec(memory_space=pltpu.SMEM),
            pl.BlockSpec(memory_space=pl.ANY),
            pl.BlockSpec(memory_space=pltpu.VMEM),
        ],
        out_specs=[pl.BlockSpec(memory_space=pltpu.VMEM)] * 2,
        out_shape=[
            pltpu.VMEM(codes.shape, jnp.bfloat16),
            pltpu.VMEM(marks_shape, jnp.float32),
        ],
        scratch_shapes=[
            pltpu.VMEM(scales.shape, jnp.float32),
            pltpu.SemaphoreType.DMA((codes.shape[1] // BLOCK,)),
        ],
        compiler_params=pltpu.CompilerParams(vmem_limit_bytes=12 * 1024 * 1024),
    )(mask, codes, in_vmem(scales))


def pairs(move, places, ratio):
    out = []
    for plane in range(places):
        for half in range(ratio):
            for place in range(places):
                p, h, q = move(plane, half, place)
                out.append(
                    ((plane * ratio + half) * places + place, (p * ratio + h) * places + q)
                )
    return out


def after(x, earlier):
    return lax.optimization_barrier((x, earlier))[0]


def shuffle_kernel(order, write, index_ref, *refs):
    count = len(order)
    choices, outs = refs[:count], refs[-1:] if write else refs[-count:]
    for i in range(count):
        for j, choice in zip(order, choices):

            @pl.when(index_ref[0] == i ^ j)
            def _():
                if write:
                    write(outs[0], i, choice[...])
                else:
                    outs[i][...] = choice[...]


def shuffle(choices, index, earlier=(), shape=None, write=None):
    one = choices[0]
    shapes = [shape] if write else [one.shape] * len(choices)
    out = pl.pallas_call(
        functools.partial(shuffle_kernel, list(choices), write),
        in_specs=[pl.BlockSpec(memory_space=pltpu.SMEM)]
        + [pl.BlockSpec(memory_space=pltpu.VMEM)] * len(choices)
        + [pl.BlockSpec(memory_space=pl.ANY)] * len(earlier),
        out_specs=[pl.BlockSpec(memory_space=pltpu.VMEM)] * len(shapes),
        out_shape=[pltpu.VMEM(s, one.dtype) for s in shapes],
        compiler_params=pltpu.CompilerParams(vmem_limit_bytes=16 * 1024 * 1024),
    )(index, *[in_vmem(x) for x in choices.values()], *earlier)
    return out[0] if write else list(out)


def own_half_kernel(first, half_ref, x_ref, w_ref, out_ref):
    _, places, chunk, _ = out_ref.shape
    feats = x_ref.shape[2]
    at = pl.ds(pl.multiple_of(half_ref[0] * feats, feats), feats)
    flat = x_ref[:, pl.ds(first, chunk), :].reshape(places * chunk, feats)
    for g in range(2):
        out_ref[g] = jnp.dot(flat, w_ref[g, at, :], preferred_element_type=jnp.float32).reshape(
            out_ref.shape[1:]
        )


def own_half(x, w_gu, half, first, chunk):
    places = x.shape[0]
    return pl.pallas_call(
        functools.partial(own_half_kernel, first),
        in_specs=[pl.BlockSpec(memory_space=pltpu.SMEM)] + [pl.BlockSpec(memory_space=pltpu.VMEM)] * 2,
        out_specs=pl.BlockSpec(memory_space=pltpu.VMEM),
        out_shape=pltpu.VMEM((2, places, chunk, w_gu.shape[2]), jnp.float32),
        compiler_params=pltpu.CompilerParams(vmem_limit_bytes=12 * 1024 * 1024),
    )(half, in_vmem(x), in_vmem(w_gu))


def partial_sums_kernel(es, summed, first, chunk, aways, half_ref, *refs):
    xs, w_ref, outs = refs[: len(es)], refs[len(es)], refs[-2 * len(aways) :]
    places, _, feats = xs[0].shape
    part = chunk // len(aways)
    rows = pl.ds(first, chunk)
    for g in range(2):
        total = refs[len(es) + 1][g].reshape(places * chunk, -1) if summed else 0.0
        for e, x_ref in zip(es, xs):
            at = pl.ds(pl.multiple_of((half_ref[0] ^ e) * feats, feats), feats)
            flat = x_ref[:, rows, :].reshape(places * chunk, feats)
            total += jnp.dot(flat, w_ref[g, at, :], preferred_element_type=jnp.float32)
        for s, away in enumerate(aways):
            counts = [0, 0]
            for k in range(places):
                block = total[k * chunk + s * part : k * chunk + (s + 1) * part]
                kind = 0 if k & away else 1
                out_ref = outs[2 * s + kind]
                out_ref[g, counts[kind]] = block.astype(out_ref.dtype)
                counts[kind] += 1


def partial_sums(xs, w_gu, summed, half, first, chunk, aways):
    places, group = xs[max(xs)].shape[0], w_gu.shape[2]
    shape = (2, places // 2, chunk // len(aways), group)
    operands = [*xs.values(), w_gu, *summed]
    outs = pl.pallas_call(
        functools.partial(partial_sums_kernel, list(xs), bool(summed), first, chunk, aways),
        in_specs=[pl.BlockSpec(memory_space=pltpu.SMEM)]
        + [pl.BlockSpec(memory_space=pltpu.VMEM)] * len(operands),
        out_specs=[pl.BlockSpec(memory_space=pltpu.VMEM)] * (2 * len(aways)),
        out_shape=[pltpu.VMEM(shape, jnp.bfloat16), pltpu.VMEM(shape, jnp.float32)] * len(aways),
        compiler_params=pltpu.CompilerParams(vmem_limit_bytes=16 * 1024 * 1024),
    )(half, *[in_vmem(x) for x in operands])
    return outs[0::2], outs[1::2]


def input_grad_kernel(spots, es, first, count, half_ref, *refs):
    pieces, w_ref = refs[: len(spots)], refs[len(spots)]
    d_ref, *term_refs = refs[len(refs) - 1 - len(es) :]
    for piece, row in zip(pieces, spots):
        streams, _, part, _ = piece.shape
        for s in range(streams):
            d_ref[:, pl.ds(row + s * part, part), :] = piece[s]
    mine = pl.ds(first, count)
    numbers = (((1,), (1,)), ((), ()))
    for e, term_ref in zip(es, term_refs):
        feats = term_ref.shape[1]
        at = pl.ds(pl.multiple_of((half_ref[0] ^ e) * feats, feats), feats)
        term = lax.dot_general(
            d_ref[0, mine, :], w_ref[0, at, :], numbers, preferred_element_type=jnp.float32
        ) + lax.dot_general(
            d_ref[1, mine, :], w_ref[1, at, :], numbers, preferred_element_type=jnp.float32
        )
        term_ref[mine, :] = term.astype(jnp.bfloat16)


def input_grad(pieces, spots, w_gu, half, es, ratio, total, first, count, earlier, filled=()):
    _, owned, group = w_gu.shape
    feats = owned // ratio
    operands = [half, *[in_vmem(x) for x in pieces], in_vmem(w_gu), *earlier, *[in_vmem(x) for x in filled]]
    return pl.pallas_call(
        functools.partial(input_grad_kernel, spots, es, first, count),
        in_specs=[pl.BlockSpec(memory_space=pltpu.SMEM)]
        + [pl.BlockSpec(memory_space=pltpu.VMEM)] * (len(pieces) + 1)
        + [pl.BlockSpec(memory_space=pl.ANY)] * len(earlier)
        + [pl.BlockSpec(memory_space=pltpu.VMEM)] * len(filled),
        out_specs=[pl.BlockSpec(memory_space=pltpu.VMEM)] * (len(es) + 1),
        out_shape=[pltpu.VMEM((2, total, group), jnp.bfloat16)]
        + [pltpu.VMEM((total, feats), jnp.bfloat16)] * len(es),
        input_output_aliases={len(operands) - len(filled) + i: i for i in range(len(filled))},
        compiler_params=pltpu.CompilerParams(vmem_limit_bytes=16 * 1024 * 1024),
    )(*operands)


def weight_grad_kernel(scale, features_ref, d_ref, mask_ref, *refs):
    out_ref, marks_ref = refs[-2:]
    mark(marks_ref, mask_ref)
    out_ref[0] = scale * lax.dot_general(
        features_ref[...], d_ref[0], (((0,), (0,)), ((), ())), preferred_element_type=jnp.float32
    )


def weight_grad(first, count, features, d_both, scale, mask, marks_shape, earlier, grads=None):
    total, owned = features.shape
    group = d_both.shape[2]
    step = min(owned, GRAD_ROWS)
    parts = owned // step
    operands = [features, in_vmem(d_both), mask, earlier] + ([] if grads is None else [grads])
    return pl.pallas_call(
        functools.partial(weight_grad_kernel, scale),
        grid=(count,),
        in_specs=[
            pl.BlockSpec((total, step), lambda i: (0, (first + i) % parts)),
            pl.BlockSpec((1, total, group), lambda i: ((first + i) // parts, 0, 0)),
            pl.BlockSpec(memory_space=pltpu.SMEM),
        ]
        + [pl.BlockSpec(memory_space=pl.ANY)] * (len(operands) - 3),
        out_specs=[
            pl.BlockSpec((1, step, group), lambda i: ((first + i) // parts, (first + i) % parts, 0)),
            pl.BlockSpec(marks_shape, lambda i: (0, 0)),
        ],
        out_shape=[
            jax.ShapeDtypeStruct((2, owned, group), jnp.float32),
            pltpu.VMEM(marks_shape, jnp.float32),
        ],
        input_output_aliases={} if grads is None else {4: 0},
        compiler_params=pltpu.CompilerParams(vmem_limit_bytes=16 * 1024 * 1024),
    )(*operands)


def body(tokens, gate_up_codes, gate_up_scales, d_hidden):
    rows, feats = tokens.shape
    nodes, places = lax.axis_size("node"), lax.axis_size("local")
    ratio = nodes // places
    _, owned, group = gate_up_codes.shape
    bits = [1 << b for b in range(places.bit_length() - 1)]
    node, place = lax.axis_index("node"), lax.axis_index("local")
    tokens, half, mask = lax.optimization_barrier(
        (tokens, (node & (ratio - 1))[None], ((node >> (ratio.bit_length() - 1)) ^ place)[None])
    )
    chunk = rows // CHUNKS
    part = chunk // 2
    orders = (bits, bits[::-1])

    def permute(x, move):
        return lax.ppermute(x, AXES, pairs(move, places, ratio))

    def own_features(x, marks):
        got = {j: permute(x, lambda p, h, q: (q ^ j, h, p)) for j in [*range(1, places), 0]}
        return jnp.stack([pick(got, k, marks) for k in range(places)])

    def joined(halves):
        def by_half(out_ref, i, value):
            for c in range(CHUNKS):
                out_ref[c, :, :, i * feats : (i + 1) * feats] = value[:, c * chunk : (c + 1) * chunk]

        return shuffle(dict(enumerate(halves)), half, (), (CHUNKS, places, chunk, owned), by_half)

    def sent(x, order, step):
        ks = [k for k in range(places) if not any(k & bit for bit in order[:step])]
        bit = order[step]
        away = [i for i, k in enumerate(ks) if k & bit]
        stay = [i for i, k in enumerate(ks) if not k & bit]
        out = jnp.stack([x[:, i] for i in away], axis=1).astype(jnp.bfloat16)
        keep = jnp.stack([x[:, i] for i in stay], axis=1).astype(jnp.float32)
        return keep, permute(out, lambda p, h, q: (p, h, q ^ bit))

    def start_forward(c, early):
        aways = [order[0] for order in orders]
        xs = dict(enumerate([mine] + others))
        summed = [own_half(xs.pop(0), w_gu, half, c * chunk, chunk)] if early else []
        out, keep = partial_sums(xs, w_gu, summed, half, c * chunk, chunk, aways)
        return keep, [
            permute(x, lambda p, h, q, bit=bit: (p, h, q ^ bit)) for x, bit in zip(out, aways)
        ]

    def next_sums(keep, got, step):
        summed = [k + g.astype(jnp.float32) for k, g in zip(keep, got)]
        return list(zip(*[sent(x, orders[s], step) for s, x in enumerate(summed)]))

    def gradients(keep, got, first):
        hidden, streams = [], []
        for k, g in zip(keep, got):
            gate, up = (k + g.astype(jnp.float32))[:, 0]
            sigmoid_gate = jax.nn.sigmoid(gate)
            active = gate * sigmoid_gate
            hidden.append((active * up).astype(jnp.bfloat16))
            grad_in = d_hidden[first : first + gate.shape[0]].astype(jnp.float32)
            first += gate.shape[0]
            d_gate = grad_in * up * sigmoid_gate * (1.0 + gate * (1.0 - sigmoid_gate))
            d_up = grad_in * active
            streams.append(jnp.stack([d_gate, d_up]).astype(jnp.bfloat16))
        return hidden, jnp.stack(streams)

    def send_direct(x):
        return {bit: permute(x, lambda p, h, q: (p, h, q ^ bit)) for bit in bits}

    def forward_rest(c, x, direct):
        pieces, spots = [x] + [direct[bit] for bit in bits], [(c * places + k) * chunk for k in [0] + bits]
        for s, order in enumerate(orders):
            held = {0: None}
            for bit in order:
                for k in list(held):
                    if k == 0:
                        held[bit] = direct[bit][s : s + 1]
                    else:
                        held[k ^ bit] = permute(held[k], lambda p, h, q: (p, h, q ^ bit))
                        pieces.append(held[k ^ bit])
                        spots.append((c * places + (k ^ bit)) * chunk + s * part)
        return pieces, spots

    w_gu, marks = dequant(gate_up_codes, gate_up_scales, mask, (places, feats))
    mine = own_features(tokens, marks)
    others = [permute(mine, lambda p, h, q, e=e: (p, h ^ e, q)) for e in range(1, ratio)]
    (keep_a, got_a), (keep_b, got_b) = start_forward(0, False), start_forward(1, True)
    for step in range(1, len(bits)):
        keep_a, got_a = next_sums(keep_a, got_a, step)
        keep_b, got_b = next_sums(keep_b, got_b, step)
    hidden_b, streams_b = gradients(keep_b, got_b, chunk)
    hidden_a, streams_a = gradients(keep_a, after(got_a, streams_b), 0)
    direct_a, direct_b = send_direct(streams_a), send_direct(streams_b)
    pieces_a, spots_a = forward_rest(0, streams_a, direct_a)
    pieces_b, spots_b = forward_rest(1, streams_b, direct_b)
    near, total, count = 1 + len(bits), places * rows, places * chunk
    d_all, own_term, *other_terms = input_grad(
        pieces_b + pieces_a[:near],
        spots_b + spots_a[:near],
        w_gu, half, list(range(ratio)), ratio, total, count, count, hidden_a + hidden_b,
    )
    d_all, *other_terms = input_grad(
        pieces_a[near:],
        spots_a[near:],
        w_gu, half, list(range(1, ratio)), ratio, total, 0, count, [], [d_all, *other_terms],
    )
    d_all, own_term = input_grad([], [], w_gu, half, [0], ratio, total, 0, count, [], [d_all, own_term])
    summed = own_term.astype(jnp.float32)
    for e, term in enumerate(other_terms, 1):
        got = permute(term, lambda p, h, q: (p, h ^ e, q))
        summed = summed + got.astype(jnp.float32)
    summed = summed.reshape(CHUNKS, places, chunk, feats).astype(jnp.bfloat16)
    summed = [summed[:, k].reshape(rows, feats) for k in range(places)]
    far_first = [*range(places // 2, places), *range(1, places // 2)]
    arrived = {k: permute(summed[k], lambda p, h, q: (p, h, q ^ k)) for k in range(1, places)}
    arrived[0] = summed[0]
    flat = joined([mine] + others).reshape(total, owned)
    scale = 1.0 / math.sqrt(rows * places)
    blocks = 2 * (owned // min(owned, GRAD_ROWS))
    early = max(1, 2 * blocks // 8)
    grads, marks = weight_grad(0, early, flat, d_all, scale, mask, marks.shape, summed[0][:16])
    arrived = [pick(arrived, j, marks) for j in range(places)]
    summands = [arrived[0]] + [
        permute(arrived[j], lambda p, h, q: (p ^ j, h, q)) for j in reversed(far_first)
    ]
    grads, marks = weight_grad(
        early, blocks - early, flat, d_all, scale, mask, marks.shape, arrived[0][:16], grads
    )
    summands[0] = after(summands[0], marks)
    d_tokens = sum(x.astype(jnp.float32) for x in summands).astype(jnp.bfloat16)
    return jnp.concatenate(hidden_a + hidden_b), d_tokens, grads


def solution(mesh):
    placed = (
        P("local", "node"),
        P(None, "local", "node"),
        P(None, "local", "node"),
        P("local", "node"),
    )
    return jax.shard_map(
        body,
        mesh=mesh,
        in_specs=placed,
        out_specs=(P("local", "node"), P("local", "node"), P(None, "local", "node")),
        check_vma=False,
    )
```

```python
import functools
import math

import jax
import jax.numpy as jnp
from jax import lax
from jax.experimental import pallas as pl
from jax.experimental.pallas import tpu as pltpu
from jax.sharding import PartitionSpec as P

BLOCK = 128
CHUNKS = 2
AXES = ("node", "local")


def in_vmem(x):
    return pltpu.with_memory_space_constraint(x, pltpu.VMEM)


def mark(marks_ref, mask_ref):
    for i in range(marks_ref.shape[0]):
        marks_ref[i : i + 1, :] = jnp.where(mask_ref[0] == i, 1.0, 0.0) * jnp.ones_like(marks_ref[:1, :])


def pick(choices, i, marks):
    out = choices[i]
    for m in reversed(range(1, len(choices))):
        out = jnp.where(marks[m : m + 1] > 0.5, choices[i ^ m], out)
    return out


def dequant_kernel(mask_ref, codes_ref, scales_ref, w_ref, marks_ref, wide_ref, sem):
    mark(marks_ref, mask_ref)
    _, owned, group = w_ref.shape
    tile = 16

    def copy(b):
        at = pl.ds(b * BLOCK, BLOCK)
        return pltpu.make_async_copy(codes_ref.at[:, at, :], w_ref.at[:, at, :], sem.at[b])

    for b in range(owned // BLOCK):
        copy(b).start()
    wide_ref[...] = scales_ref[...].astype(jnp.float32)
    for b in range(owned // BLOCK):
        copy(b).wait()
        for g in range(2):
            scale = jnp.broadcast_to(wide_ref[g, b : b + 1, :], (tile, group)).astype(jnp.bfloat16)
            for t in range(b * BLOCK, (b + 1) * BLOCK, tile):
                w_ref[g, t : t + tile] = w_ref[g, t : t + tile] * scale


def dequant(codes, scales, mask, marks_shape):
    codes = pltpu.with_memory_space_constraint(codes, pltpu.HBM)
    return pl.pallas_call(
        dequant_kernel,
        in_specs=[
            pl.BlockSpec(memory_space=pltpu.SMEM),
            pl.BlockSpec(memory_space=pl.ANY),
            pl.BlockSpec(memory_space=pltpu.VMEM),
        ],
        out_specs=[pl.BlockSpec(memory_space=pltpu.VMEM)] * 2,
        out_shape=[
            pltpu.VMEM(codes.shape, jnp.bfloat16),
            pltpu.VMEM(marks_shape, jnp.float32),
        ],
        scratch_shapes=[
            pltpu.VMEM(scales.shape, jnp.float32),
            pltpu.SemaphoreType.DMA((codes.shape[1] // BLOCK,)),
        ],
        compiler_params=pltpu.CompilerParams(vmem_limit_bytes=12 * 1024 * 1024),
    )(mask, codes, in_vmem(scales))


def pairs(move, places, ratio):
    out = []
    for plane in range(places):
        for half in range(ratio):
            for place in range(places):
                p, h, q = move(plane, half, place)
                out.append(
                    ((plane * ratio + half) * places + place, (p * ratio + h) * places + q)
                )
    return out


def after(x, earlier):
    return lax.optimization_barrier((x, earlier))[0]


def shuffle_kernel(order, write, index_ref, *refs):
    count = len(order)
    choices, outs = refs[:count], refs[-1:] if write else refs[-count:]
    for i in range(count):
        for j, choice in zip(order, choices):

            @pl.when(index_ref[0] == i ^ j)
            def _():
                if write:
                    write(outs[0], i, choice[...])
                else:
                    outs[i][...] = choice[...]


def shuffle(choices, index, earlier=(), shape=None, write=None):
    one = choices[0]
    shapes = [shape] if write else [one.shape] * len(choices)
    out = pl.pallas_call(
        functools.partial(shuffle_kernel, list(choices), write),
        in_specs=[pl.BlockSpec(memory_space=pltpu.SMEM)]
        + [pl.BlockSpec(memory_space=pltpu.VMEM)] * len(choices)
        + [pl.BlockSpec(memory_space=pl.ANY)] * len(earlier),
        out_specs=[pl.BlockSpec(memory_space=pltpu.VMEM)] * len(shapes),
        out_shape=[pltpu.VMEM(s, one.dtype) for s in shapes],
        compiler_params=pltpu.CompilerParams(vmem_limit_bytes=16 * 1024 * 1024),
    )(index, *[in_vmem(x) for x in choices.values()], *earlier)
    return out[0] if write else list(out)


def own_half_kernel(first, half_ref, x_ref, w_ref, out_ref):
    _, places, chunk, _ = out_ref.shape
    feats = x_ref.shape[2]
    at = pl.ds(pl.multiple_of(half_ref[0] * feats, feats), feats)
    flat = x_ref[:, pl.ds(first, chunk), :].reshape(places * chunk, feats)
    for g in range(2):
        out_ref[g] = jnp.dot(flat, w_ref[g, at, :], preferred_element_type=jnp.float32).reshape(
            out_ref.shape[1:]
        )


def own_half(x, w_gu, half, first, chunk):
    places = x.shape[0]
    return pl.pallas_call(
        functools.partial(own_half_kernel, first),
        in_specs=[pl.BlockSpec(memory_space=pltpu.SMEM)] + [pl.BlockSpec(memory_space=pltpu.VMEM)] * 2,
        out_specs=pl.BlockSpec(memory_space=pltpu.VMEM),
        out_shape=pltpu.VMEM((2, places, chunk, w_gu.shape[2]), jnp.float32),
        compiler_params=pltpu.CompilerParams(vmem_limit_bytes=12 * 1024 * 1024),
    )(half, in_vmem(x), in_vmem(w_gu))


def partial_sums_kernel(es, summed, first, chunk, aways, half_ref, *refs):
    xs, w_ref, outs = refs[: len(es)], refs[len(es)], refs[-2 * len(aways) :]
    places, _, feats = xs[0].shape
    part = chunk // len(aways)
    rows = pl.ds(first, chunk)
    for g in range(2):
        total = refs[len(es) + 1][g].reshape(places * chunk, -1) if summed else 0.0
        for e, x_ref in zip(es, xs):
            at = pl.ds(pl.multiple_of((half_ref[0] ^ e) * feats, feats), feats)
            flat = x_ref[:, rows, :].reshape(places * chunk, feats)
            total += jnp.dot(flat, w_ref[g, at, :], preferred_element_type=jnp.float32)
        for s, away in enumerate(aways):
            counts = [0, 0]
            for k in range(places):
                block = total[k * chunk + s * part : k * chunk + (s + 1) * part]
                kind = 0 if k & away else 1
                out_ref = outs[2 * s + kind]
                out_ref[g, counts[kind]] = block.astype(out_ref.dtype)
                counts[kind] += 1


def partial_sums(xs, w_gu, summed, half, first, chunk, aways):
    places, group = xs[max(xs)].shape[0], w_gu.shape[2]
    shape = (2, places // 2, chunk // len(aways), group)
    operands = [*xs.values(), w_gu, *summed]
    outs = pl.pallas_call(
        functools.partial(partial_sums_kernel, list(xs), bool(summed), first, chunk, aways),
        in_specs=[pl.BlockSpec(memory_space=pltpu.SMEM)]
        + [pl.BlockSpec(memory_space=pltpu.VMEM)] * len(operands),
        out_specs=[pl.BlockSpec(memory_space=pltpu.VMEM)] * (2 * len(aways)),
        out_shape=[pltpu.VMEM(shape, jnp.bfloat16), pltpu.VMEM(shape, jnp.float32)] * len(aways),
        compiler_params=pltpu.CompilerParams(vmem_limit_bytes=16 * 1024 * 1024),
    )(half, *[in_vmem(x) for x in operands])
    return outs[0::2], outs[1::2]


def input_grad_kernel(spots, es, first, count, half_ref, *refs):
    pieces, w_ref = refs[: len(spots)], refs[len(spots)]
    d_ref, *term_refs = refs[len(refs) - 1 - len(es) :]
    for piece, row in zip(pieces, spots):
        streams, _, part, _ = piece.shape
        for s in range(streams):
            d_ref[:, pl.ds(row + s * part, part), :] = piece[s]
    mine = pl.ds(first, count)
    numbers = (((1,), (1,)), ((), ()))
    for e, term_ref in zip(es, term_refs):
        feats = term_ref.shape[1]
        at = pl.ds(pl.multiple_of((half_ref[0] ^ e) * feats, feats), feats)
        term = lax.dot_general(
            d_ref[0, mine, :], w_ref[0, at, :], numbers, preferred_element_type=jnp.float32
        ) + lax.dot_general(
            d_ref[1, mine, :], w_ref[1, at, :], numbers, preferred_element_type=jnp.float32
        )
        term_ref[mine, :] = term.astype(jnp.bfloat16)


def input_grad(pieces, spots, w_gu, half, es, ratio, total, first, count, earlier, filled=()):
    _, owned, group = w_gu.shape
    feats = owned // ratio
    operands = [half, *[in_vmem(x) for x in pieces], in_vmem(w_gu), *earlier, *[in_vmem(x) for x in filled]]
    return pl.pallas_call(
        functools.partial(input_grad_kernel, spots, es, first, count),
        in_specs=[pl.BlockSpec(memory_space=pltpu.SMEM)]
        + [pl.BlockSpec(memory_space=pltpu.VMEM)] * (len(pieces) + 1)
        + [pl.BlockSpec(memory_space=pl.ANY)] * len(earlier)
        + [pl.BlockSpec(memory_space=pltpu.VMEM)] * len(filled),
        out_specs=[pl.BlockSpec(memory_space=pltpu.VMEM)] * (len(es) + 1),
        out_shape=[pltpu.VMEM((2, total, group), jnp.bfloat16)]
        + [pltpu.VMEM((total, feats), jnp.bfloat16)] * len(es),
        input_output_aliases={len(operands) - len(filled) + i: i for i in range(len(filled))},
        compiler_params=pltpu.CompilerParams(vmem_limit_bytes=16 * 1024 * 1024),
    )(*operands)


def weight_grad_kernel(scale, features_ref, d_ref, mask_ref, *refs):
    out_ref, marks_ref = refs[-2:]
    mark(marks_ref, mask_ref)
    out_ref[0] = scale * lax.dot_general(
        features_ref[...], d_ref[0], (((0,), (0,)), ((), ())), preferred_element_type=jnp.float32
    )


def weight_grad(which, features, d_both, scale, mask, marks_shape, earlier, grads=None):
    total, owned = features.shape
    group = d_both.shape[2]
    step = min(owned, 256)
    operands = [features, in_vmem(d_both), mask, earlier] + ([] if grads is None else [grads])
    return pl.pallas_call(
        functools.partial(weight_grad_kernel, scale),
        grid=(owned // step,),
        in_specs=[
            pl.BlockSpec((total, step), lambda i: (0, i)),
            pl.BlockSpec((1, total, group), lambda i: (which, 0, 0)),
            pl.BlockSpec(memory_space=pltpu.SMEM),
        ]
        + [pl.BlockSpec(memory_space=pl.ANY)] * (len(operands) - 3),
        out_specs=[
            pl.BlockSpec((1, step, group), lambda i: (which, i, 0)),
            pl.BlockSpec(marks_shape, lambda i: (0, 0)),
        ],
        out_shape=[
            jax.ShapeDtypeStruct((2, owned, group), jnp.float32),
            pltpu.VMEM(marks_shape, jnp.float32),
        ],
        input_output_aliases={} if grads is None else {4: 0},
        compiler_params=pltpu.CompilerParams(vmem_limit_bytes=16 * 1024 * 1024),
    )(*operands)


def body(tokens, gate_up_codes, gate_up_scales, d_hidden):
    rows, feats = tokens.shape
    nodes, places = lax.axis_size("node"), lax.axis_size("local")
    ratio = nodes // places
    _, owned, group = gate_up_codes.shape
    bits = [1 << b for b in range(places.bit_length() - 1)]
    node, place = lax.axis_index("node"), lax.axis_index("local")
    tokens, half, mask = lax.optimization_barrier(
        (tokens, (node & (ratio - 1))[None], ((node >> (ratio.bit_length() - 1)) ^ place)[None])
    )
    chunk = rows // CHUNKS
    part = chunk // 2
    orders = (bits, bits[::-1])

    def permute(x, move):
        return lax.ppermute(x, AXES, pairs(move, places, ratio))

    def own_features(x, marks):
        got = {j: permute(x, lambda p, h, q: (q ^ j, h, p)) for j in [*range(1, places), 0]}
        return jnp.stack([pick(got, k, marks) for k in range(places)])

    def joined(halves):
        def by_half(out_ref, i, value):
            for c in range(CHUNKS):
                out_ref[c, :, :, i * feats : (i + 1) * feats] = value[:, c * chunk : (c + 1) * chunk]

        return shuffle(dict(enumerate(halves)), half, (), (CHUNKS, places, chunk, owned), by_half)

    def sent(x, order, step):
        ks = [k for k in range(places) if not any(k & bit for bit in order[:step])]
        bit = order[step]
        away = [i for i, k in enumerate(ks) if k & bit]
        stay = [i for i, k in enumerate(ks) if not k & bit]
        out = jnp.stack([x[:, i] for i in away], axis=1).astype(jnp.bfloat16)
        keep = jnp.stack([x[:, i] for i in stay], axis=1).astype(jnp.float32)
        return keep, permute(out, lambda p, h, q: (p, h, q ^ bit))

    def start_forward(c, early):
        aways = [order[0] for order in orders]
        xs = dict(enumerate([mine] + others))
        summed = [own_half(xs.pop(0), w_gu, half, c * chunk, chunk)] if early else []
        out, keep = partial_sums(xs, w_gu, summed, half, c * chunk, chunk, aways)
        return keep, [
            permute(x, lambda p, h, q, bit=bit: (p, h, q ^ bit)) for x, bit in zip(out, aways)
        ]

    def next_sums(keep, got, step):
        summed = [k + g.astype(jnp.float32) for k, g in zip(keep, got)]
        return list(zip(*[sent(x, orders[s], step) for s, x in enumerate(summed)]))

    def gradients(keep, got, first):
        hidden, streams = [], []
        for k, g in zip(keep, got):
            gate, up = (k + g.astype(jnp.float32))[:, 0]
            sigmoid_gate = jax.nn.sigmoid(gate)
            active = gate * sigmoid_gate
            hidden.append((active * up).astype(jnp.bfloat16))
            grad_in = d_hidden[first : first + gate.shape[0]].astype(jnp.float32)
            first += gate.shape[0]
            d_gate = grad_in * up * sigmoid_gate * (1.0 + gate * (1.0 - sigmoid_gate))
            d_up = grad_in * active
            streams.append(jnp.stack([d_gate, d_up]).astype(jnp.bfloat16))
        return hidden, jnp.stack(streams)

    def send_direct(x):
        return {bit: permute(x, lambda p, h, q: (p, h, q ^ bit)) for bit in bits}

    def forward_rest(c, x, direct):
        pieces, spots = [x] + [direct[bit] for bit in bits], [(c * places + k) * chunk for k in [0] + bits]
        for s, order in enumerate(orders):
            held = {0: None}
            for bit in order:
                for k in list(held):
                    if k == 0:
                        held[bit] = direct[bit][s : s + 1]
                    else:
                        held[k ^ bit] = permute(held[k], lambda p, h, q: (p, h, q ^ bit))
                        pieces.append(held[k ^ bit])
                        spots.append((c * places + (k ^ bit)) * chunk + s * part)
        return pieces, spots

    w_gu, marks = dequant(gate_up_codes, gate_up_scales, mask, (places, feats))
    mine = own_features(tokens, marks)
    others = [permute(mine, lambda p, h, q, e=e: (p, h ^ e, q)) for e in range(1, ratio)]
    (keep_a, got_a), (keep_b, got_b) = start_forward(0, False), start_forward(1, True)
    for step in range(1, len(bits)):
        keep_a, got_a = next_sums(keep_a, got_a, step)
        keep_b, got_b = next_sums(keep_b, got_b, step)
    hidden_b, streams_b = gradients(keep_b, got_b, chunk)
    hidden_a, streams_a = gradients(keep_a, after(got_a, streams_b), 0)
    direct_a, direct_b = send_direct(streams_a), send_direct(streams_b)
    pieces_a, spots_a = forward_rest(0, streams_a, direct_a)
    pieces_b, spots_b = forward_rest(1, streams_b, direct_b)
    near, total, count = 1 + len(bits), places * rows, places * chunk
    d_all, own_term, *other_terms = input_grad(
        pieces_b + pieces_a[:near],
        spots_b + spots_a[:near],
        w_gu, half, list(range(ratio)), ratio, total, count, count, hidden_b + hidden_a,
    )
    d_all, *other_terms = input_grad(
        pieces_a[near:],
        spots_a[near:],
        w_gu, half, list(range(1, ratio)), ratio, total, 0, count, [], [d_all, *other_terms],
    )
    d_all, own_term = input_grad([], [], w_gu, half, [0], ratio, total, 0, count, [], [d_all, own_term])
    summed = own_term.astype(jnp.float32)
    for e, term in enumerate(other_terms, 1):
        got = permute(term, lambda p, h, q: (p, h ^ e, q))
        summed = summed + got.astype(jnp.float32)
    summed = summed.reshape(CHUNKS, places, chunk, feats).astype(jnp.bfloat16)
    summed = [summed[:, k].reshape(rows, feats) for k in range(places)]
    far_first = [*range(places // 2, places), *range(1, places // 2)]
    arrived = {k: permute(summed[k], lambda p, h, q: (p, h, q ^ k)) for k in range(1, places)}
    arrived[0] = summed[0]
    flat = joined([mine] + others).reshape(total, owned)
    scale = 1.0 / math.sqrt(rows * places)
    grads, marks = weight_grad(0, flat, d_all, scale, mask, marks.shape, summed[0][:16])
    arrived = [pick(arrived, j, marks) for j in range(places)]
    summands = [arrived[0]] + [
        permute(arrived[j], lambda p, h, q: (p ^ j, h, q)) for j in reversed(far_first)
    ]
    grads, marks = weight_grad(1, flat, d_all, scale, mask, marks.shape, arrived[0][:16], grads)
    summands[0] = after(summands[0], marks)
    d_tokens = sum(x.astype(jnp.float32) for x in summands).astype(jnp.bfloat16)
    return jnp.concatenate(hidden_a + hidden_b), d_tokens, grads


def solution(mesh):
    placed = (
        P("local", "node"),
        P(None, "local", "node"),
        P(None, "local", "node"),
        P("local", "node"),
    )
    return jax.shard_map(
        body,
        mesh=mesh,
        in_specs=placed,
        out_specs=(P("local", "node"), P("local", "node"), P(None, "local", "node")),
        check_vma=False,
    )
```
